512 devices in a mesh: seq: 128 (over z, x_lo, y), head: 4 (over x_hi, core).
Axes of the slice: x: 4 (x_hi: 2, x_lo: 2; x = x_hi * 2 + x_lo), y: 4, z: 16, core: 2. Of those that a mesh axis runs over, the one named last changes fastest.
Arguments:
- frames_in: bfloat16 [32768, 1024], P(('seq', 'head')), may hold values from -12 to 12
- query_weight: bfloat16 [1024, 1024], P(None, 'head'), may hold values from -0.1875 to 0.1875
- key_weight: bfloat16 [1024, 1024], P(None, 'head'), may hold values from -0.1875 to 0.1875
- value_weight: bfloat16 [1024, 1024], P(None, 'head'), may hold values from -0.1875 to 0.1875
- out_weight: bfloat16 [1024, 1024], P('head'), may hold values from -0.1875 to 0.1875
- read_mask: int32 [128, 3], replicated, may hold values from 0 to 1, as said below
- out_grad: bfloat16 [32768, 1024], P(('seq', 'head')), may hold values from -24 to 24
Outputs:
- mixed: bfloat16 [32768, 1024], P(('seq', 'head'))
- frames_grad: bfloat16 [32768, 1024], P(('seq', 'head'))
- grad_value_weight: float32 [1024, 1024], P('seq', 'head')
- grad_out_weight: float32 [1024, 1024], P('head', 'seq')
The draws below stay inside these ranges and needn't reach their ends.
Inputs may be any that keep to these rules, and one draw needn't show every extreme that they name: read_mask[i, k - 1] is 1 only where stretch i - k exists and lies in the same dialogue as stretch i.
All inputs are finite; a program needn't handle non-finite values.
Results may differ from the reference program's by a relative error of at most 0.023.
The reference program's roundings to bfloat16 on the way (of `weights_soft`, `attended`, `out_back`, `score_grad` and `query_grad`) count: a program that leaves them out, or rounds other values in their place, can miss the bound.
Values may be sent and summed in bfloat16 or wider, within the bound.
No kernel may reach another device: no remote copies, remote signals or barrier semaphores. Data moves between devices by JAX's collectives and lax.ppermute only.
A program may use at most 64 MiB of HBM per device.

```python
import jax
import jax.numpy as jnp
from jax import lax

WIDTH = 1024
HEADS = 16
HEAD_DIM = 64
STRETCH = 256
WINDOW = 4
STRETCHES = 128
FRAMES = 32768
FEATURES = 1024
N_HEAD = 4


def draw_frames_in(key, part):
    key = jax.random.fold_in(key, 11)
    first = jax.random.fold_in(key, 0)
    values = jnp.clip(jax.random.normal(first, (FRAMES, WIDTH), jnp.float32), -6.0, 6.0)
    return values.astype(jnp.bfloat16)


def draw_read_mask(key, part):
    key = jax.random.fold_in(key, 23)
    first, second = jax.random.split(key, 2)
    starts = jax.random.randint(first, (STRETCHES,), 0, 3) == 0
    starts = starts.at[0].set(True)
    dialog = jnp.cumsum(starts.astype(jnp.int32))
    turns = jax.random.randint(second, (STRETCHES, WINDOW - 1), 0, 4) > 0
    index = jnp.arange(STRETCHES, dtype=jnp.int32)[:, None]
    earlier = index - jnp.arange(1, WINDOW, dtype=jnp.int32)[None, :]
    same = (earlier >= 0) & (dialog[jnp.maximum(earlier, 0)] == dialog[:, None])
    return (same & turns).astype(jnp.int32)


def raised(result, rng, source, target, blocks, factor):
    def block_of(position):
        return (jnp.arange(result.shape[position]) // (result.shape[position] // blocks)).reshape((-1,) + (1,) * (result.ndim - 1 - position))

    near = jax.random.permutation(rng, blocks)[block_of(target)]
    other_side = (block_of(target) + blocks // 2) % blocks
    return jnp.where((block_of(source) == near) | (block_of(source) == other_side), factor * result, result)


def level_of(rng, dims, cuts, smallest, largest):
    loudness = 1.0
    for axis_at, shards_of in cuts:
        heights = jax.random.uniform(jax.random.fold_in(jax.random.fold_in(rng, 6), axis_at), (shards_of,), jnp.float32, smallest / len(cuts), largest / len(cuts))
        loudness = loudness * jnp.repeat(jnp.exp(heights), dims[axis_at] // shards_of).reshape((-1,) + (1,) * (len(dims) - 1 - axis_at))
    return loudness


def gaussian(rng, dims, deviation, bound, shards=(), kind=jnp.bfloat16):
    array = jax.random.normal(rng, dims, jnp.float32) * deviation
    if len(shards) > 0:
        array = level_of(rng, dims, shards, -0.22, 0.18) * array
    return jnp.clip(array, min=-bound, max=bound).astype(kind)


def noise_with(own_key, extent, width, reach, cuts, heavy, held_as=jnp.bfloat16):
    array = width * jax.random.normal(own_key, extent, jnp.float32)
    if cuts:
        array = array * level_of(own_key, extent, cuts, -0.22, 0.18)
    return jnp.clip(raised(array, jax.random.fold_in(own_key, 3), *heavy), -reach, reach).astype(held_as)


def setup_inputs(seed: int = 0) -> dict:
    key_of = jax.random.split(jax.random.key(seed), 8)
    return {
        "frames_in": draw_frames_in(jax.random.fold_in(key_of[7], 71), 0),
        "query_weight": gaussian(key_of[1], (WIDTH, FEATURES), WIDTH ** -0.5, 0.1875, ((1, 4),)),
        "key_weight": gaussian(key_of[2], (WIDTH, FEATURES), WIDTH ** -0.5, 0.1875, ((1, 4),)),
        "value_weight": gaussian(key_of[3], (WIDTH, FEATURES), WIDTH ** -0.5, 0.1875, ((1, 4),)),
        "out_weight": gaussian(key_of[4], (FEATURES, WIDTH), FEATURES ** -0.5, 0.1875, ((0, 4),)),
        "read_mask": draw_read_mask(jax.random.fold_in(key_of[7], 71), 0),
        "out_grad": noise_with(key_of[6], (FRAMES, WIDTH), 1.0, 24.0, ((0, 512),), (0, 1, 512, 6.0)),
    }


def blocks_of(tensor, index):
    parts = [tensor[index]]
    for distance in range(1, WINDOW):
        parts.append(tensor[jnp.maximum(index - distance, 0)])
    return jnp.concatenate(parts, axis=0)


def keep_of(read_mask, index):
    flags = [jnp.ones((STRETCH,), jnp.bool_)]
    for distance in range(1, WINDOW):
        flags.append(jnp.broadcast_to(read_mask[index, distance - 1] > 0, (STRETCH,)))
    return jnp.concatenate(flags)


def scores_of(query_rows, key_rows, keep):
    factor = HEAD_DIM ** -0.5
    scores = jnp.einsum("qhe,khe->hqk", query_rows.astype(jnp.float32), key_rows.astype(jnp.float32)) * factor
    return jnp.where(keep[None, None, :], scores, -1e30)


def group_sum(pairs):
    total = jnp.zeros((FRAMES, WIDTH), jnp.float32)
    share = FEATURES // N_HEAD
    for group in range(N_HEAD):
        term = jnp.zeros((FRAMES, WIDTH), jnp.float32)
        for left, right in pairs:
            term = term + jnp.dot(left[:, group * share:(group + 1) * share], right[:, group * share:(group + 1) * share].T, preferred_element_type=jnp.float32)
        rounded = lax.optimization_barrier(term.astype(jnp.bfloat16))
        total = total + rounded.astype(jnp.float32)
    return total.astype(jnp.bfloat16)


def reference(frames_in, query_weight, key_weight, value_weight, out_weight, read_mask, out_grad):
    factor = HEAD_DIM ** -0.5
    queries = jnp.dot(frames_in, query_weight, preferred_element_type=jnp.float32).astype(jnp.bfloat16)
    keys = jnp.dot(frames_in, key_weight, preferred_element_type=jnp.float32).astype(jnp.bfloat16)
    values = jnp.dot(frames_in, value_weight, preferred_element_type=jnp.float32).astype(jnp.bfloat16)
    query_stretches = queries.reshape(STRETCHES, STRETCH, HEADS, HEAD_DIM)
    key_stretches = keys.reshape(STRETCHES, STRETCH, HEADS, HEAD_DIM)
    value_stretches = values.reshape(STRETCHES, STRETCH, HEADS, HEAD_DIM)
    indices = jnp.arange(STRETCHES, dtype=jnp.int32)

    def forward_stretch(index):
        scores = scores_of(query_stretches[index], blocks_of(key_stretches, index), keep_of(read_mask, index))
        top = jnp.max(scores, axis=-1)
        log_total = top + jnp.log(jnp.sum(jnp.exp(scores - top[..., None]), axis=-1))
        weights_soft = jnp.exp(scores - log_total[..., None]).astype(jnp.bfloat16)
        output = jnp.einsum("hqk,khe->qhe", weights_soft.astype(jnp.float32), blocks_of(value_stretches, index).astype(jnp.float32))
        return output.astype(jnp.bfloat16), log_total

    attended_stretches, total_stretches = lax.map(forward_stretch, indices)
    attended = attended_stretches.reshape(FRAMES, FEATURES)
    mixed = group_sum([(attended, out_weight.T)])

    out_back = jnp.dot(out_grad, out_weight.T, preferred_element_type=jnp.float32).astype(jnp.bfloat16)
    back_stretches = out_back.reshape(STRETCHES, STRETCH, HEADS, HEAD_DIM)
    dot_stretches = jnp.sum(back_stretches.astype(jnp.float32) * attended_stretches.astype(jnp.float32), axis=-1)

    def backward_stretch(carry, index):
        key_acc, value_acc = carry
        query_rows = query_stretches[index]
        back_rows = back_stretches[index]
        key_rows = blocks_of(key_stretches, index)
        value_rows = blocks_of(value_stretches, index)
        keep = keep_of(read_mask, index)
        scores = scores_of(query_rows, key_rows, keep)
        weights_full = jnp.exp(scores - total_stretches[index][..., None])
        weights_soft = weights_full.astype(jnp.bfloat16)
        back_scores = jnp.einsum("qhe,khe->hqk", back_rows.astype(jnp.float32), value_rows.astype(jnp.float32))
        back_scores = jnp.where(keep[None, None, :], back_scores, 0.0)
        back_dot = jnp.transpose(dot_stretches[index])
        score_grad = (weights_full * (back_scores - back_dot[..., None]) * factor).astype(jnp.bfloat16)
        query_grad = jnp.einsum("hqk,khe->qhe", score_grad.astype(jnp.float32), key_rows.astype(jnp.float32)).astype(jnp.bfloat16)
        key_part = jnp.einsum("hqk,qhe->khe", score_grad.astype(jnp.float32), query_rows.astype(jnp.float32))
        value_part = jnp.einsum("hqk,qhe->khe", weights_soft.astype(jnp.float32), back_rows.astype(jnp.float32))
        for distance in range(WINDOW):
            target = jnp.maximum(index - distance, 0)
            key_acc = key_acc.at[target].add(key_part[distance * STRETCH:(distance + 1) * STRETCH])
            value_acc = value_acc.at[target].add(value_part[distance * STRETCH:(distance + 1) * STRETCH])
        return (key_acc, value_acc), query_grad

    empty = jnp.zeros((STRETCHES, STRETCH, HEADS, HEAD_DIM), jnp.float32)
    (key_acc, value_acc), query_grads = lax.scan(backward_stretch, (empty, empty), indices)
    query_grad = query_grads.reshape(FRAMES, FEATURES)
    key_grad = key_acc.reshape(FRAMES, FEATURES).astype(jnp.bfloat16)
    value_grad = value_acc.reshape(FRAMES, FEATURES).astype(jnp.bfloat16)
    frames_grad = group_sum([(query_grad, query_weight), (key_grad, key_weight), (value_grad, value_weight)])
    grad_value_weight = jnp.dot(frames_in.T, value_grad, preferred_element_type=jnp.float32)
    grad_out_weight = jnp.dot(attended.T, out_grad, preferred_element_type=jnp.float32)
    return mixed, frames_grad, grad_value_weight, grad_out_weight
```

```python
import functools

import jax
import jax.numpy as jnp
from jax import lax
from jax.experimental import pallas as pl
from jax.experimental.pallas import tpu as pltpu
from jax.sharding import PartitionSpec as P

HEAD_DIM = 64
WINDOW = 4
FAR = 1e30
VMEM_LIMIT = 48 * 1024 * 1024

F32 = jnp.float32
BF16 = jnp.bfloat16


def dot_nn(left, right):
    return jnp.dot(left, right, preferred_element_type=F32)


def dot_nt(left, right):
    return lax.dot_general(left, right, (((1,), (1,)), ((), ())), preferred_element_type=F32)


def dot_tn(left, right):
    return lax.dot_general(left, right, (((0,), (0,)), ((), ())), preferred_element_type=F32)


def turned(array):
    return jnp.transpose(array.astype(F32)).astype(BF16)


def call(kernel, outs, operands, scratch=(), smem=0, flops=0, transcendentals=0):
    specs = [pl.BlockSpec(memory_space=pltpu.SMEM)] * smem
    specs += [pl.BlockSpec(memory_space=pltpu.VMEM)] * (len(operands) - smem)
    touched = sum(o.size * o.dtype.itemsize for o in (*operands, *outs))
    return pl.pallas_call(
        kernel,
        out_shape=outs,
        in_specs=specs,
        out_specs=[pl.BlockSpec(memory_space=pltpu.VMEM)] * len(outs),
        scratch_shapes=list(scratch),
        compiler_params=pltpu.CompilerParams(vmem_limit_bytes=VMEM_LIMIT),
        cost_estimate=pl.CostEstimate(
            flops=flops, bytes_accessed=touched, transcendentals=transcendentals
        ),
    )(*operands)


def shape_of(shape, dtype):
    return jax.ShapeDtypeStruct(shape, dtype)


def head_rows(array, head):
    rows = lax.broadcasted_iota(jnp.int32, array.shape, 0)
    inside = (rows >= head * HEAD_DIM) & (rows < (head + 1) * HEAD_DIM)
    return jnp.where(inside, array, jnp.zeros_like(array))


def kv_kernel(frames_ref, key_weight_ref, value_weight_ref, kv_ref):
    span = key_weight_ref.shape[1]
    kv_ref[:, :span] = dot_nn(frames_ref[...], key_weight_ref[...]).astype(BF16)
    kv_ref[:, span:] = dot_nn(frames_ref[...], value_weight_ref[...]).astype(BF16)


def query_kernel(frames_ref, grads_ref, query_weight_ref, out_weight_ref, qt_ref, back_ref):
    queries = dot_nn(frames_ref[...], query_weight_ref[...]).astype(BF16).astype(F32)
    qt_ref[...] = (jnp.transpose(queries) * (HEAD_DIM**-0.5)).astype(BF16)
    back_ref[...] = dot_nt(out_weight_ref[...], grads_ref[...]).astype(BF16)


def relay_kernel(head_ref, before_ref, after_ref, relay_ref):
    odd = lax.rem(head_ref[0], 2) == 1

    @pl.when(odd)
    def _():
        relay_ref[...] = after_ref[...]

    @pl.when(jnp.logical_not(odd))
    def _():
        relay_ref[...] = before_ref[...]


def attention_kernel(
    mask_ref, qt_ref, bt_ref, kv0, kv1, kv2, kv3, att_ref, dq_ref, own_ref, far1, far2, far3,
    soft, grad, back_stack, query_stack, att_t, dq_t,
):
    kvs = (kv0, kv1, kv2, kv3)
    span, count = qt_ref.shape
    heads = span // HEAD_DIM
    keep = [None] + [mask_ref[0, k] > 0 for k in range(WINDOW - 1)]
    keys_t = [turned(kv[:, :span]) for kv in kvs]
    values_t = [turned(kv[:, span:]) for kv in kvs]
    for head in range(heads):
        mine = slice(head * HEAD_DIM, (head + 1) * HEAD_DIM)
        lanes = slice(head * count, (head + 1) * count)
        query = head_rows(qt_ref[...], head)
        back = head_rows(bt_ref[...], head)
        query_stack[:, lanes] = query
        back_stack[:, lanes] = back
        scores = [dot_nn(kv[:, :span], query) for kv in kvs]
        top = jnp.max(scores[0], axis=0, keepdims=True)
        for k in range(1, WINDOW):
            block_top = jnp.max(scores[k], axis=0, keepdims=True)
            top = jnp.maximum(top, jnp.where(keep[k], block_top, -FAR))
        raised = [jnp.exp(scores[0] - top)]
        for k in range(1, WINDOW):
            raised.append(jnp.exp(scores[k] - jnp.where(keep[k], top, FAR)))
        total = sum(jnp.sum(part, axis=0, keepdims=True) for part in raised)
        inverse = 1.0 / total
        weights = [part * inverse for part in raised]
        out = jnp.zeros((HEAD_DIM, count), F32)
        for k in range(WINDOW):
            rounded = weights[k].astype(BF16)
            soft[k, :, lanes] = rounded
            out = out + dot_nn(values_t[k][mine, :], rounded)
        out = out.astype(BF16).astype(F32)
        att_t[mine, :] = out
        back_dot = jnp.sum(out * bt_ref[mine, :].astype(F32), axis=0, keepdims=True)
        out = jnp.zeros((HEAD_DIM, count), F32)
        for k in range(WINDOW):
            back_scores = dot_nn(kvs[k][:, span:], back)
            score_grad = (weights[k] * (back_scores - back_dot)).astype(BF16)
            grad[k, :, lanes] = score_grad
            out = out + dot_nn(keys_t[k][mine, :], score_grad)
        dq_t[mine, :] = out * (HEAD_DIM**-0.5)
    for k, far in ((1, far1), (2, far2), (3, far3)):
        far[:, :span] = dot_nt(grad[k], query_stack[...]).astype(BF16)
        far[:, span:] = dot_nt(soft[k], back_stack[...]).astype(BF16)
    own_ref[:, :span] = dot_nt(grad[0], query_stack[...])
    own_ref[:, span:] = dot_nt(soft[0], back_stack[...])
    att_ref[...] = jnp.transpose(att_t[...]).astype(BF16)
    dq_ref[...] = jnp.transpose(dq_t[...]).astype(BF16)


def shares(head_ref, term, outs):
    half = outs[0].shape[0]
    for other, out in enumerate(outs):
        start = pl.multiple_of(jnp.bitwise_xor(head_ref[0], other) * half, half)
        out[...] = term[pl.ds(start, half), :].astype(BF16)


def added(parts):
    total = parts[0][...].astype(F32)
    for part in parts[1:]:
        total = total + part[...].astype(F32)
    return total


def mix_kernel(head_ref, att_ref, out_weight_ref, grads_ref, own_ref, send1, send2, send3, term_ref, held):
    held[...] = dot_nn(att_ref[...], out_weight_ref[...])
    shares(head_ref, held, (own_ref, send1, send2, send3))
    term_ref[...] = dot_tn(grads_ref[...], att_ref[...])


def weights_kernel(
    cuts, frames_ref, own_ref, far1, far2, far3, out_term_ref, part0, part1, part2, part3,
    kv_grad_ref, terms_ref, mixed_ref,
):
    outer, inner, tail = cuts
    rounded = added((own_ref, far1, far2, far3)).astype(BF16)
    kv_grad_ref[...] = rounded
    span = rounded.shape[1] // 2
    value_term = dot_tn(frames_ref[...], rounded[:, span:]).reshape(outer, inner, tail, span)
    out_term = out_term_ref[...].reshape(outer, inner, tail, span)
    for i in range(inner):
        piece = jnp.stack([value_term[:, i], out_term[:, i]], axis=1)
        terms_ref[i] = piece.reshape(2 * outer * tail, span).astype(BF16)
    mixed_ref[...] = added((part0, part1, part2, part3)).astype(BF16)


def input_kernel(
    head_ref, dq_ref, kv_grad_ref, query_weight_ref, key_weight_ref, value_weight_ref,
    own_ref, send1, send2, send3, held,
):
    span = dq_ref.shape[1]
    term = dot_nt(dq_ref[...], query_weight_ref[...])
    term = term + dot_nt(kv_grad_ref[:, :span], key_weight_ref[...])
    held[...] = term + dot_nt(kv_grad_ref[:, span:], value_weight_ref[...])
    shares(head_ref, held, (own_ref, send1, send2, send3))


def near_kernel(pieces_ref, part0, part1, part2, part3, terms_ref, frames_grad_ref):
    terms_ref[...] = added([pieces_ref.at[i] for i in range(pieces_ref.shape[0])]).astype(BF16)
    frames_grad_ref[...] = added((part0, part1, part2, part3)).astype(BF16)


def far_kernel(pieces_ref, value_ref, out_ref):
    total = added([pieces_ref.at[i] for i in range(pieces_ref.shape[0])])
    rows = value_ref.shape[0]
    value_ref[...] = total[:rows]
    out_ref[...] = total[rows:]


def passed_along(value, steps):
    count = lax.axis_size("seq")
    return lax.ppermute(value, "seq", [(i, (i + steps) % count) for i in range(count)])


def relayed(value):
    count, groups = lax.axis_size("seq"), lax.axis_size("head")
    pairs = []
    for i in range(count):
        for group in range(groups):
            to = (i + (1 if group % 2 == 0 else -1)) % count
            pairs.append((i * groups + group, to * groups + group))
    return lax.ppermute(value, ("seq", "head"), pairs)


def exchanged(sends):
    count = lax.axis_size("head")
    received = {}
    for other in range(count - 1, 0, -1):
        pairs = [(i, i ^ other) for i in range(count)]
        received[other] = lax.ppermute(sends[other - 1], "head", pairs)
    return [received[other] for other in range(1, count)]


def per_device(inner, frames_in, query_weight, key_weight, value_weight, out_weight, read_mask, out_grad):
    seq = lax.axis_size("seq")
    groups = lax.axis_size("head")
    outer = seq // inner
    width, span = query_weight.shape
    tail = width // seq
    near = [[o * inner + i for i in range(inner)] for o in range(outer)]
    across = [[o * inner + i for o in range(outer)] for i in range(inner)]
    mask = lax.dynamic_slice_in_dim(read_mask, lax.axis_index("seq"), 1, 0)
    group = jnp.full((1,), lax.axis_index("head"), jnp.int32)

    share = frames_in.shape[0]
    count = groups * share
    square = 2 * count * span
    heads = span // HEAD_DIM
    pairs = heads * WINDOW * count * count
    side = shape_of((span, count), BF16)
    shared = [shape_of((share, width), BF16)] * groups
    held = pltpu.VMEM((count, width), F32)

    frames = lax.all_gather(frames_in, "head", axis=0, tiled=True)
    kv_shape = shape_of((count, 2 * span), BF16)
    [kv] = call(kv_kernel, [kv_shape], [frames, key_weight, value_weight], flops=2 * square * width)
    kv3 = passed_along(kv, 3)
    kv1 = passed_along(kv, 1)
    grads = lax.all_gather(out_grad, "head", axis=0, tiled=True)
    [relay] = call(relay_kernel, [kv_shape], [group, kv1, kv3], smem=1)
    kv2 = relayed(relay)
    qt, bt = call(
        query_kernel,
        [side, side],
        [frames, grads, query_weight, out_weight],
        flops=2 * square * width,
    )
    attended, dq, own, *fars = call(
        attention_kernel,
        [shape_of((count, span), BF16)] * 2
        + [shape_of((count, 2 * span), F32)]
        + [kv_shape] * (WINDOW - 1),
        [mask, qt, bt, kv, kv1, kv2, kv3],
        [pltpu.VMEM((WINDOW, count, heads * count), BF16)] * 2
        + [pltpu.VMEM((span, heads * count), BF16)] * 2
        + [pltpu.VMEM((span, count), F32)] * 2,
        smem=1,
        flops=12 * pairs * span,
        transcendentals=pairs,
    )
    fars = [passed_along(fars[k - 1], -k) for k in range(1, WINDOW)]
    kept, *sends, out_term = call(
        mix_kernel,
        [*shared, shape_of((width, span), F32)],
        [group, attended, out_weight, grads],
        [held],
        smem=1,
        flops=2 * square * width,
    )
    kv_grad, terms, mixed = call(
        functools.partial(weights_kernel, (outer, inner, tail)),
        [kv_shape, shape_of((inner, 2 * outer * tail, span), BF16), shared[0]],
        [frames, own, *fars, out_term, kept, *exchanged(sends)],
        flops=square * width,
    )
    terms = lax.all_to_all(terms, "seq", 0, 0, axis_index_groups=near, tiled=True)
    kept, *sends = call(
        input_kernel,
        shared,
        [group, dq, kv_grad, query_weight, key_weight, value_weight],
        [held],
        smem=1,
        flops=3 * square * width,
    )
    terms, frames_grad = call(
        near_kernel,
        [shape_of((2 * outer * tail, span), BF16), shared[0]],
        [terms, kept, *exchanged(sends)],
    )
    terms = terms.reshape(outer, 2 * tail, span)
    terms = lax.all_to_all(terms, "seq", 0, 0, axis_index_groups=across, tiled=True)
    value_sum, out_sum = call(far_kernel, [shape_of((tail, span), F32)] * 2, [terms])
    return mixed, frames_grad, value_sum, out_sum.T


def solution(mesh):
    in_specs = (
        P(("seq", "head"), None),
        P(None, "head"),
        P(None, "head"),
        P(None, "head"),
        P("head", None),
        P(),
        P(("seq", "head"), None),
    )
    out_specs = (
        P(("seq", "head"), None),
        P(("seq", "head"), None),
        P("seq", "head"),
        P("head", "seq"),
    )
    return jax.shard_map(
        functools.partial(per_device, min(8, mesh.shape["seq"])),
        mesh=mesh,
        in_specs=in_specs,
        out_specs=out_specs,
        check_vma=False,
    )
```

```python
import functools

import jax
import jax.numpy as jnp
from jax import lax
from jax.experimental import pallas as pl
from jax.experimental.pallas import tpu as pltpu
from jax.sharding import PartitionSpec as P

HEAD_DIM = 64
WINDOW = 4
FAR = 1e30
VMEM_LIMIT = 24 * 1024 * 1024

F32 = jnp.float32
BF16 = jnp.bfloat16


def dot_nn(left, right):
    return jnp.dot(left, right, preferred_element_type=F32)


def dot_nt(left, right):
    return lax.dot_general(left, right, (((1,), (1,)), ((), ())), preferred_element_type=F32)


def dot_tn(left, right):
    return lax.dot_general(left, right, (((0,), (0,)), ((), ())), preferred_element_type=F32)


def turned(array):
    return jnp.transpose(array.astype(F32)).astype(BF16)


def call(kernel, outs, operands, scratch=(), smem=0, flops=0, transcendentals=0):
    specs = [pl.BlockSpec(memory_space=pltpu.SMEM)] * smem
    specs += [pl.BlockSpec(memory_space=pltpu.VMEM)] * (len(operands) - smem)
    touched = sum(o.size * o.dtype.itemsize for o in (*operands, *outs))
    return pl.pallas_call(
        kernel,
        out_shape=outs,
        in_specs=specs,
        out_specs=[pl.BlockSpec(memory_space=pltpu.VMEM)] * len(outs),
        scratch_shapes=list(scratch),
        compiler_params=pltpu.CompilerParams(vmem_limit_bytes=VMEM_LIMIT),
        cost_estimate=pl.CostEstimate(
            flops=flops, bytes_accessed=touched, transcendentals=transcendentals
        ),
    )(*operands)


def shape_of(shape, dtype):
    return jax.ShapeDtypeStruct(shape, dtype)


def head_rows(array, head):
    rows = lax.broadcasted_iota(jnp.int32, array.shape, 0)
    inside = (rows >= head * HEAD_DIM) & (rows < (head + 1) * HEAD_DIM)
    return jnp.where(inside, array, jnp.zeros_like(array))


def kv_kernel(frames_ref, key_weight_ref, value_weight_ref, kv_ref):
    span = key_weight_ref.shape[1]
    kv_ref[:, :span] = dot_nn(frames_ref[...], key_weight_ref[...]).astype(BF16)
    kv_ref[:, span:] = dot_nn(frames_ref[...], value_weight_ref[...]).astype(BF16)


def query_kernel(frames_ref, grads_ref, query_weight_ref, out_weight_ref, qt_ref, back_ref):
    queries = dot_nn(frames_ref[...], query_weight_ref[...]).astype(BF16).astype(F32)
    qt_ref[...] = (jnp.transpose(queries) * (HEAD_DIM**-0.5)).astype(BF16)
    back_ref[...] = dot_nt(out_weight_ref[...], grads_ref[...]).astype(BF16)


def attention_kernel(
    mask_ref, qt_ref, bt_ref, kv0, kv1, kv2, kv3, att_ref, dq_ref, own_ref, far1, far2, far3,
    soft, grad, back_stack, query_stack, att_t, dq_t,
):
    kvs = (kv0, kv1, kv2, kv3)
    span, count = qt_ref.shape
    heads = span // HEAD_DIM
    keep = [None] + [mask_ref[0, k] > 0 for k in range(WINDOW - 1)]
    keys_t = [turned(kv[:, :span]) for kv in kvs]
    values_t = [turned(kv[:, span:]) for kv in kvs]
    for head in range(heads):
        mine = slice(head * HEAD_DIM, (head + 1) * HEAD_DIM)
        lanes = slice(head * count, (head + 1) * count)
        query = head_rows(qt_ref[...], head)
        back = head_rows(bt_ref[...], head)
        query_stack[:, lanes] = query
        back_stack[:, lanes] = back
        scores = [dot_nn(kv[:, :span], query) for kv in kvs]
        top = jnp.max(scores[0], axis=0, keepdims=True)
        for k in range(1, WINDOW):
            block_top = jnp.max(scores[k], axis=0, keepdims=True)
            top = jnp.maximum(top, jnp.where(keep[k], block_top, -FAR))
        raised = [jnp.exp(scores[0] - top)]
        for k in range(1, WINDOW):
            raised.append(jnp.exp(scores[k] - jnp.where(keep[k], top, FAR)))
        total = sum(jnp.sum(part, axis=0, keepdims=True) for part in raised)
        inverse = 1.0 / total
        weights = [part * inverse for part in raised]
        out = jnp.zeros((HEAD_DIM, count), F32)
        for k in range(WINDOW):
            rounded = weights[k].astype(BF16)
            soft[k, :, lanes] = rounded
            out = out + dot_nn(values_t[k][mine, :], rounded)
        out = out.astype(BF16).astype(F32)
        att_t[mine, :] = out
        back_dot = jnp.sum(out * bt_ref[mine, :].astype(F32), axis=0, keepdims=True)
        out = jnp.zeros((HEAD_DIM, count), F32)
        for k in range(WINDOW):
            back_scores = dot_nn(kvs[k][:, span:], back)
            score_grad = (weights[k] * (back_scores - back_dot)).astype(BF16)
            grad[k, :, lanes] = score_grad
            out = out + dot_nn(keys_t[k][mine, :], score_grad)
        dq_t[mine, :] = out * (HEAD_DIM**-0.5)
    for k, far in ((1, far1), (2, far2), (3, far3)):
        far[:, :span] = dot_nt(grad[k], query_stack[...]).astype(BF16)
        far[:, span:] = dot_nt(soft[k], back_stack[...]).astype(BF16)
    own_ref[:, :span] = dot_nt(grad[0], query_stack[...])
    own_ref[:, span:] = dot_nt(soft[0], back_stack[...])
    att_ref[...] = jnp.transpose(att_t[...]).astype(BF16)
    dq_ref[...] = jnp.transpose(dq_t[...]).astype(BF16)


def added(parts):
    total = parts[0][...].astype(F32)
    for part in parts[1:]:
        total = total + part[...].astype(F32)
    return total


def weights_kernel(cuts, frames_ref, grads_ref, att_ref, own_ref, far1, far2, far3, kv_grad_ref, terms_ref):
    outer, inner, tail = cuts
    rounded = added((own_ref, far1, far2, far3)).astype(BF16)
    kv_grad_ref[...] = rounded
    span = rounded.shape[1] // 2
    value_term = dot_tn(frames_ref[...], rounded[:, span:]).reshape(outer, inner, tail, span)
    out_term = dot_tn(grads_ref[...], att_ref[...]).reshape(outer, inner, tail, span)
    for i in range(inner):
        piece = jnp.stack([value_term[:, i], out_term[:, i]], axis=1)
        terms_ref[i] = piece.reshape(2 * outer * tail, span).astype(BF16)


def shares(head_ref, term, outs):
    half = outs[0].shape[0]
    for other, out in enumerate(outs):
        start = pl.multiple_of(jnp.bitwise_xor(head_ref[0], other) * half, half)
        out[...] = term[pl.ds(start, half), :].astype(BF16)


def input_kernel(
    head_ref, dq_ref, kv_grad_ref, query_weight_ref, key_weight_ref, value_weight_ref, att_ref, out_weight_ref,
    own_ref, send1, send2, send3, mixed_own_ref, mixed_send1, mixed_send2, mixed_send3, held_mixed, held,
):
    span = dq_ref.shape[1]
    held_mixed[...] = dot_nn(att_ref[...], out_weight_ref[...])
    term = dot_nt(dq_ref[...], query_weight_ref[...])
    term = term + dot_nt(kv_grad_ref[:, :span], key_weight_ref[...])
    held[...] = term + dot_nt(kv_grad_ref[:, span:], value_weight_ref[...])
    shares(head_ref, held, (own_ref, send1, send2, send3))
    shares(head_ref, held_mixed, (mixed_own_ref, mixed_send1, mixed_send2, mixed_send3))


def near_kernel(pieces_ref, part0, part1, part2, part3, terms_ref, frames_grad_ref):
    terms_ref[...] = added([pieces_ref.at[i] for i in range(pieces_ref.shape[0])]).astype(BF16)
    frames_grad_ref[...] = added((part0, part1, part2, part3)).astype(BF16)


def far_kernel(pieces_ref, value_ref, out_ref):
    total = added([pieces_ref.at[i] for i in range(pieces_ref.shape[0])])
    rows = value_ref.shape[0]
    value_ref[...] = total[:rows]
    out_ref[...] = total[rows:]


def mixed_kernel(part0, part1, part2, part3, mixed_ref):
    mixed_ref[...] = added((part0, part1, part2, part3)).astype(BF16)


def passed_along(value, steps):
    count = lax.axis_size("seq")
    first, last = max(0, -steps), min(count, count - steps)
    return lax.ppermute(value, "seq", [(i, i + steps) for i in range(first, last)])


def exchanged(sends):
    count = lax.axis_size("head")
    received = {}
    for other in range(count - 1, 0, -1):
        pairs = [(i, i ^ other) for i in range(count)]
        received[other] = lax.ppermute(sends[other - 1], "head", pairs)
    return [received[other] for other in range(1, count)]


def per_device(inner, frames_in, query_weight, key_weight, value_weight, out_weight, read_mask, out_grad):
    seq = lax.axis_size("seq")
    groups = lax.axis_size("head")
    outer = seq // inner
    width, span = query_weight.shape
    tail = width // seq
    near = [[o * inner + i for i in range(inner)] for o in range(outer)]
    across = [[o * inner + i for o in range(outer)] for i in range(inner)]
    mask = lax.dynamic_slice_in_dim(read_mask, lax.axis_index("seq"), 1, 0)
    group = jnp.full((1,), lax.axis_index("head"), jnp.int32)

    share = frames_in.shape[0]
    count = groups * share
    square = 2 * count * span
    heads = span // HEAD_DIM
    pairs = heads * WINDOW * count * count
    side = shape_of((span, count), BF16)
    kv_shape = shape_of((count, 2 * span), BF16)
    held = pltpu.VMEM((count, width), F32)

    frames = lax.all_gather(frames_in, "head", axis=0, tiled=True)
    [kv] = call(kv_kernel, [kv_shape], [frames, key_weight, value_weight], flops=2 * square * width)
    kvs = [kv] + [passed_along(kv, steps) for steps in range(1, WINDOW)]
    grads = lax.all_gather(out_grad, "head", axis=0, tiled=True)
    qt, bt = call(
        query_kernel,
        [side, side],
        [frames, grads, query_weight, out_weight],
        flops=2 * square * width,
    )
    attended, dq, own, *fars = call(
        attention_kernel,
        [shape_of((count, span), BF16)] * 2
        + [shape_of((count, 2 * span), F32)]
        + [kv_shape] * (WINDOW - 1),
        [mask, qt, bt, *kvs],
        [pltpu.VMEM((WINDOW, count, heads * count), BF16)] * 2
        + [pltpu.VMEM((span, heads * count), BF16)] * 2
        + [pltpu.VMEM((span, count), F32)] * 2,
        smem=1,
        flops=12 * pairs * span,
        transcendentals=pairs,
    )
    fars = [passed_along(fars[k - 1], -k) for k in range(1, WINDOW)]
    kv_grad, terms = call(
        functools.partial(weights_kernel, (outer, inner, tail)),
        [kv_shape, shape_of((inner, 2 * outer * tail, span), BF16)],
        [frames, grads, attended, own, *fars],
        flops=2 * square * width,
    )
    terms = lax.all_to_all(terms, "seq", 0, 0, axis_index_groups=near, tiled=True)
    shared = shape_of((share, width), BF16)
    sends = call(
        input_kernel,
        [shared] * (2 * groups),
        [group, dq, kv_grad, query_weight, key_weight, value_weight, attended, out_weight],
        [held, held],
        smem=1,
        flops=4 * square * width,
    )
    frames_parts = [sends[0], *exchanged(sends[1:groups])]
    mixed_parts = [sends[groups], *exchanged(sends[groups + 1 :])]
    terms, frames_grad = call(
        near_kernel,
        [shape_of((2 * outer * tail, span), BF16), shared],
        [terms, *frames_parts],
    )
    terms = terms.reshape(outer, 2 * tail, span)
    terms = lax.all_to_all(terms, "seq", 0, 0, axis_index_groups=across, tiled=True)
    [mixed] = call(mixed_kernel, [shared], mixed_parts)
    value_sum, out_sum = call(far_kernel, [shape_of((tail, span), F32)] * 2, [terms])
    return mixed, frames_grad, value_sum, out_sum.T


def solution(mesh):
    in_specs = (
        P(("seq", "head"), None),
        P(None, "head"),
        P(None, "head"),
        P(None, "head"),
        P("head", None),
        P(),
        P(("seq", "head"), None),
    )
    out_specs = (
        P(("seq", "head"), None),
        P(("seq", "head"), None),
        P("seq", "head"),
        P("head", "seq"),
    )
    return jax.shard_map(
        functools.partial(per_device, min(8, mesh.shape["seq"])),
        mesh=mesh,
        in_specs=in_specs,
        out_specs=out_specs,
        check_vma=False,
    )
```

```python
import functools

import jax
import jax.numpy as jnp
from jax import lax
from jax.experimental import pallas as pl
from jax.experimental.pallas import tpu as pltpu
from jax.sharding import PartitionSpec as P

HEAD_DIM = 64
WINDOW = 4
FAR = 1e30
VMEM_LIMIT = 24 * 1024 * 1024

F32 = jnp.float32
BF16 = jnp.bfloat16


def dot_nn(left, right):
    return jnp.dot(left, right, preferred_element_type=F32)


def dot_nt(left, right):
    return lax.dot_general(left, right, (((1,), (1,)), ((), ())), preferred_element_type=F32)


def dot_tn(left, right):
    return lax.dot_general(left, right, (((0,), (0,)), ((), ())), preferred_element_type=F32)


def turned(array):
    return jnp.transpose(array.astype(F32)).astype(BF16)


def call(kernel, outs, operands, scratch=(), smem=0, flops=0, transcendentals=0):
    specs = [pl.BlockSpec(memory_space=pltpu.SMEM)] * smem
    specs += [pl.BlockSpec(memory_space=pltpu.VMEM)] * (len(operands) - smem)
    touched = sum(o.size * o.dtype.itemsize for o in (*operands, *outs))
    return pl.pallas_call(
        kernel,
        out_shape=outs,
        in_specs=specs,
        out_specs=[pl.BlockSpec(memory_space=pltpu.VMEM)] * len(outs),
        scratch_shapes=list(scratch),
        compiler_params=pltpu.CompilerParams(vmem_limit_bytes=VMEM_LIMIT),
        cost_estimate=pl.CostEstimate(
            flops=flops, bytes_accessed=touched, transcendentals=transcendentals
        ),
    )(*operands)


def shape_of(shape, dtype):
    return jax.ShapeDtypeStruct(shape, dtype)


def head_rows(array, head):
    rows = lax.broadcasted_iota(jnp.int32, array.shape, 0)
    inside = (rows >= head * HEAD_DIM) & (rows < (head + 1) * HEAD_DIM)
    return jnp.where(inside, array, jnp.zeros_like(array))


def kv_kernel(frames_ref, key_weight_ref, value_weight_ref, kv_ref):
    span = key_weight_ref.shape[1]
    kv_ref[:, :span] = dot_nn(frames_ref[...], key_weight_ref[...]).astype(BF16)
    kv_ref[:, span:] = dot_nn(frames_ref[...], value_weight_ref[...]).astype(BF16)


def query_kernel(
    frames_ref, grads_ref, query_weight_ref, out_weight_ref, kv_ref, qt_ref, back_ref, again_ref
):
    again_ref[...] = kv_ref[...]
    queries = dot_nn(frames_ref[...], query_weight_ref[...]).astype(BF16).astype(F32)
    qt_ref[...] = (jnp.transpose(queries) * (HEAD_DIM**-0.5)).astype(BF16)
    back_ref[...] = dot_nt(out_weight_ref[...], grads_ref[...]).astype(BF16)


def attention_kernel(
    mask_ref, qt_ref, bt_ref, kv0, kv1, kv2, kv3, att_ref, dq_ref, own_ref, far1, far2, far3,
    soft, grad, back_stack, query_stack, att_t, dq_t,
):
    kvs = (kv0, kv1, kv2, kv3)
    span, count = qt_ref.shape
    heads = span // HEAD_DIM
    keep = [None] + [mask_ref[0, k] > 0 for k in range(WINDOW - 1)]
    keys_t = [turned(kv[:, :span]) for kv in kvs]
    values_t = [turned(kv[:, span:]) for kv in kvs]
    for head in range(heads):
        mine = slice(head * HEAD_DIM, (head + 1) * HEAD_DIM)
        lanes = slice(head * count, (head + 1) * count)
        query = head_rows(qt_ref[...], head)
        back = head_rows(bt_ref[...], head)
        query_stack[:, lanes] = query
        back_stack[:, lanes] = back
        scores = [dot_nn(kv[:, :span], query) for kv in kvs]
        top = jnp.max(scores[0], axis=0, keepdims=True)
        for k in range(1, WINDOW):
            block_top = jnp.max(scores[k], axis=0, keepdims=True)
            top = jnp.maximum(top, jnp.where(keep[k], block_top, -FAR))
        raised = [jnp.exp(scores[0] - top)]
        for k in range(1, WINDOW):
            raised.append(jnp.exp(scores[k] - jnp.where(keep[k], top, FAR)))
        total = sum(jnp.sum(part, axis=0, keepdims=True) for part in raised)
        inverse = 1.0 / total
        weights = [part * inverse for part in raised]
        out = jnp.zeros((HEAD_DIM, count), F32)
        for k in range(WINDOW):
            rounded = weights[k].astype(BF16)
            soft[k, :, lanes] = rounded
            out = out + dot_nn(values_t[k][mine, :], rounded)
        out = out.astype(BF16).astype(F32)
        att_t[mine, :] = out
        back_dot = jnp.sum(out * bt_ref[mine, :].astype(F32), axis=0, keepdims=True)
        out = jnp.zeros((HEAD_DIM, count), F32)
        for k in range(WINDOW):
            back_scores = dot_nn(kvs[k][:, span:], back)
            score_grad = (weights[k] * (back_scores - back_dot)).astype(BF16)
            grad[k, :, lanes] = score_grad
            out = out + dot_nn(keys_t[k][mine, :], score_grad)
        dq_t[mine, :] = out * (HEAD_DIM**-0.5)
    for k, far in ((1, far1), (2, far2), (3, far3)):
        far[:, :span] = dot_nt(grad[k], query_stack[...]).astype(BF16)
        far[:, span:] = dot_nt(soft[k], back_stack[...]).astype(BF16)
    own_ref[:, :span] = dot_nt(grad[0], query_stack[...])
    own_ref[:, span:] = dot_nt(soft[0], back_stack[...])
    att_ref[...] = jnp.transpose(att_t[...]).astype(BF16)
    dq_ref[...] = jnp.transpose(dq_t[...]).astype(BF16)


def added(parts):
    total = parts[0][...].astype(F32)
    for part in parts[1:]:
        total = total + part[...].astype(F32)
    return total


def weights_kernel(cuts, frames_ref, grads_ref, att_ref, own_ref, far1, far2, far3, kv_grad_ref, terms_ref):
    outer, inner, tail = cuts
    rounded = added((own_ref, far1, far2, far3)).astype(BF16)
    kv_grad_ref[...] = rounded
    span = rounded.shape[1] // 2
    value_term = dot_tn(frames_ref[...], rounded[:, span:]).reshape(outer, inner, tail, span)
    out_term = dot_tn(grads_ref[...], att_ref[...]).reshape(outer, inner, tail, span)
    for i in range(inner):
        piece = jnp.stack([value_term[:, i], out_term[:, i]], axis=1)
        terms_ref[i] = piece.reshape(2 * outer * tail, span).astype(BF16)


def shares(head_ref, term, outs):
    half = outs[0].shape[0]
    for other, out in enumerate(outs):
        start = pl.multiple_of(jnp.bitwise_xor(head_ref[0], other) * half, half)
        out[...] = term[pl.ds(start, half), :].astype(BF16)


def input_kernel(
    head_ref, dq_ref, kv_grad_ref, query_weight_ref, key_weight_ref, value_weight_ref,
    own_ref, send1, send2, send3, held,
):
    span = dq_ref.shape[1]
    term = dot_nt(dq_ref[...], query_weight_ref[...])
    term = term + dot_nt(kv_grad_ref[:, :span], key_weight_ref[...])
    held[...] = term + dot_nt(kv_grad_ref[:, span:], value_weight_ref[...])
    shares(head_ref, held, (own_ref, send1, send2, send3))


def mix_kernel(head_ref, att_ref, out_weight_ref, after_ref, own_ref, send1, send2, send3, held):
    held[...] = dot_nn(att_ref[...], out_weight_ref[...])
    shares(head_ref, held, (own_ref, send1, send2, send3))


def near_kernel(pieces_ref, part0, part1, part2, part3, terms_ref, frames_grad_ref):
    terms_ref[...] = added([pieces_ref.at[i] for i in range(pieces_ref.shape[0])]).astype(BF16)
    frames_grad_ref[...] = added((part0, part1, part2, part3)).astype(BF16)


def far_kernel(pieces_ref, value_ref, out_ref):
    total = added([pieces_ref.at[i] for i in range(pieces_ref.shape[0])])
    rows = value_ref.shape[0]
    value_ref[...] = total[:rows]
    out_ref[...] = total[rows:]


def mixed_kernel(part0, part1, part2, part3, mixed_ref):
    mixed_ref[...] = added((part0, part1, part2, part3)).astype(BF16)


def passed_along(value, steps):
    count = lax.axis_size("seq")
    first, last = max(0, -steps), min(count, count - steps)
    return lax.ppermute(value, "seq", [(i, i + steps) for i in range(first, last)])


def exchanged(sends):
    count = lax.axis_size("head")
    received = {}
    for other in range(count - 1, 0, -1):
        pairs = [(i, i ^ other) for i in range(count)]
        received[other] = lax.ppermute(sends[other - 1], "head", pairs)
    return [received[other] for other in range(1, count)]


def per_device(inner, frames_in, query_weight, key_weight, value_weight, out_weight, read_mask, out_grad):
    seq = lax.axis_size("seq")
    groups = lax.axis_size("head")
    outer = seq // inner
    width, span = query_weight.shape
    tail = width // seq
    near = [[o * inner + i for i in range(inner)] for o in range(outer)]
    across = [[o * inner + i for o in range(outer)] for i in range(inner)]
    mask = lax.dynamic_slice_in_dim(read_mask, lax.axis_index("seq"), 1, 0)
    group = jnp.full((1,), lax.axis_index("head"), jnp.int32)

    share = frames_in.shape[0]
    count = groups * share
    square = 2 * count * span
    heads = span // HEAD_DIM
    pairs = heads * WINDOW * count * count
    side = shape_of((span, count), BF16)
    kv_shape = shape_of((count, 2 * span), BF16)
    held = pltpu.VMEM((count, width), F32)

    frames = lax.all_gather(frames_in, "head", axis=0, tiled=True)
    [kv] = call(kv_kernel, [kv_shape], [frames, key_weight, value_weight], flops=2 * square * width)
    kv2 = passed_along(kv, 2)
    grads = lax.all_gather(out_grad, "head", axis=0, tiled=True)
    qt, bt, again = call(
        query_kernel,
        [side, side, kv_shape],
        [frames, grads, query_weight, out_weight, kv],
        flops=2 * square * width,
    )
    kvs = [again, passed_along(again, 1), kv2, passed_along(again, 3)]
    attended, dq, own, *fars = call(
        attention_kernel,
        [shape_of((count, span), BF16)] * 2
        + [shape_of((count, 2 * span), F32)]
        + [kv_shape] * (WINDOW - 1),
        [mask, qt, bt, *kvs],
        [pltpu.VMEM((WINDOW, count, heads * count), BF16)] * 2
        + [pltpu.VMEM((span, heads * count), BF16)] * 2
        + [pltpu.VMEM((span, count), F32)] * 2,
        smem=1,
        flops=12 * pairs * span,
        transcendentals=pairs,
    )
    fars = [passed_along(fars[k - 1], -k) for k in range(1, WINDOW)]
    kv_grad, terms = call(
        functools.partial(weights_kernel, (outer, inner, tail)),
        [kv_shape, shape_of((inner, 2 * outer * tail, span), BF16)],
        [frames, grads, attended, own, *fars],
        flops=2 * square * width,
    )
    terms = lax.all_to_all(terms, "seq", 0, 0, axis_index_groups=near, tiled=True)
    shared = shape_of((share, width), BF16)
    kept, *sends = call(
        input_kernel,
        [shared] * groups,
        [group, dq, kv_grad, query_weight, key_weight, value_weight],
        [held],
        smem=1,
        flops=3 * square * width,
    )
    terms, frames_grad = call(
        near_kernel,
        [shape_of((2 * outer * tail, span), BF16), shared],
        [terms, kept, *exchanged(sends)],
    )
    mixed_kept, *mixed_sends = call(
        mix_kernel,
        [shared] * groups,
        [group, attended, out_weight, terms],
        [held],
        smem=1,
        flops=square * width,
    )
    terms = terms.reshape(outer, 2 * tail, span)
    terms = lax.all_to_all(terms, "seq", 0, 0, axis_index_groups=across, tiled=True)
    [mixed] = call(mixed_kernel, [shared], [mixed_kept, *exchanged(mixed_sends)])
    value_sum, out_sum = call(far_kernel, [shape_of((tail, span), F32)] * 2, [terms])
    return mixed, frames_grad, value_sum, out_sum.T


def solution(mesh):
    in_specs = (
        P(("seq", "head"), None),
        P(None, "head"),
        P(None, "head"),
        P(None, "head"),
        P("head", None),
        P(),
        P(("seq", "head"), None),
    )
    out_specs = (
        P(("seq", "head"), None),
        P(("seq", "head"), None),
        P("seq", "head"),
        P("head", "seq"),
    )
    return jax.shard_map(
        functools.partial(per_device, min(8, mesh.shape["seq"])),
        mesh=mesh,
        in_specs=in_specs,
        out_specs=out_specs,
        check_vma=False,
    )
```

```python
import functools

import jax
import jax.numpy as jnp
from jax import lax
from jax.experimental import pallas as pl
from jax.experimental.pallas import tpu as pltpu
from jax.sharding import PartitionSpec as P

HEAD_DIM = 64
WINDOW = 4
FAR = 1e30
VMEM_LIMIT = 24 * 1024 * 1024

F32 = jnp.float32
BF16 = jnp.bfloat16


def dot_nn(left, right):
    return jnp.dot(left, right, preferred_element_type=F32)


def dot_nt(left, right):
    return lax.dot_general(left, right, (((1,), (1,)), ((), ())), preferred_element_type=F32)


def dot_tn(left, right):
    return lax.dot_general(left, right, (((0,), (0,)), ((), ())), preferred_element_type=F32)


def turned(array):
    return jnp.transpose(array.astype(F32)).astype(BF16)


def call(kernel, outs, operands, scratch=(), smem=0, flops=0, transcendentals=0):
    specs = [pl.BlockSpec(memory_space=pltpu.SMEM)] * smem
    specs += [pl.BlockSpec(memory_space=pltpu.VMEM)] * (len(operands) - smem)
    touched = sum(o.size * o.dtype.itemsize for o in (*operands, *outs))
    return pl.pallas_call(
        kernel,
        out_shape=outs,
        in_specs=specs,
        out_specs=[pl.BlockSpec(memory_space=pltpu.VMEM)] * len(outs),
        scratch_shapes=list(scratch),
        compiler_params=pltpu.CompilerParams(vmem_limit_bytes=VMEM_LIMIT),
        cost_estimate=pl.CostEstimate(
            flops=flops, bytes_accessed=touched, transcendentals=transcendentals
        ),
    )(*operands)


def shape_of(shape, dtype):
    return jax.ShapeDtypeStruct(shape, dtype)


def head_rows(array, head):
    rows = lax.broadcasted_iota(jnp.int32, array.shape, 0)
    inside = (rows >= head * HEAD_DIM) & (rows < (head + 1) * HEAD_DIM)
    return jnp.where(inside, array, jnp.zeros_like(array))


def kv_kernel(frames_ref, key_weight_ref, value_weight_ref, kv_ref):
    span = key_weight_ref.shape[1]
    kv_ref[:, :span] = dot_nn(frames_ref[...], key_weight_ref[...]).astype(BF16)
    kv_ref[:, span:] = dot_nn(frames_ref[...], value_weight_ref[...]).astype(BF16)


def query_kernel(frames_ref, grads_ref, query_weight_ref, out_weight_ref, qt_ref, back_ref):
    queries = dot_nn(frames_ref[...], query_weight_ref[...]).astype(BF16).astype(F32)
    qt_ref[...] = (jnp.transpose(queries) * (HEAD_DIM**-0.5)).astype(BF16)
    back_ref[...] = dot_nt(out_weight_ref[...], grads_ref[...]).astype(BF16)


def attention_kernel(
    mask_ref, qt_ref, bt_ref, kv0, kv1, kv2, kv3, att_ref, dq_ref, own_ref, far1, far2, far3,
    soft, grad, back_stack, query_stack, att_t, dq_t,
):
    kvs = (kv0, kv1, kv2, kv3)
    span, count = qt_ref.shape
    heads = span // HEAD_DIM
    keep = [None] + [mask_ref[0, k] > 0 for k in range(WINDOW - 1)]
    keys_t = [turned(kv[:, :span]) for kv in kvs]
    values_t = [turned(kv[:, span:]) for kv in kvs]
    for head in range(heads):
        mine = slice(head * HEAD_DIM, (head + 1) * HEAD_DIM)
        lanes = slice(head * count, (head + 1) * count)
        query = head_rows(qt_ref[...], head)
        back = head_rows(bt_ref[...], head)
        query_stack[:, lanes] = query
        back_stack[:, lanes] = back
        scores = [dot_nn(kv[:, :span], query) for kv in kvs]
        top = jnp.max(scores[0], axis=0, keepdims=True)
        for k in range(1, WINDOW):
            block_top = jnp.max(scores[k], axis=0, keepdims=True)
            top = jnp.maximum(top, jnp.where(keep[k], block_top, -FAR))
        raised = [jnp.exp(scores[0] - top)]
        for k in range(1, WINDOW):
            raised.append(jnp.exp(scores[k] - jnp.where(keep[k], top, FAR)))
        total = sum(jnp.sum(part, axis=0, keepdims=True) for part in raised)
        inverse = 1.0 / total
        weights = [part * inverse for part in raised]
        out = jnp.zeros((HEAD_DIM, count), F32)
        for k in range(WINDOW):
            rounded = weights[k].astype(BF16)
            soft[k, :, lanes] = rounded
            out = out + dot_nn(values_t[k][mine, :], rounded)
        out = out.astype(BF16).astype(F32)
        att_t[mine, :] = out
        back_dot = jnp.sum(out * bt_ref[mine, :].astype(F32), axis=0, keepdims=True)
        out = jnp.zeros((HEAD_DIM, count), F32)
        for k in range(WINDOW):
            back_scores = dot_nn(kvs[k][:, span:], back)
            score_grad = (weights[k] * (back_scores - back_dot)).astype(BF16)
            grad[k, :, lanes] = score_grad
            out = out + dot_nn(keys_t[k][mine, :], score_grad)
        dq_t[mine, :] = out * (HEAD_DIM**-0.5)
    for k, far in ((1, far1), (2, far2), (3, far3)):
        far[:, :span] = dot_nt(grad[k], query_stack[...]).astype(BF16)
        far[:, span:] = dot_nt(soft[k], back_stack[...]).astype(BF16)
    own_ref[:, :span] = dot_nt(grad[0], query_stack[...])
    own_ref[:, span:] = dot_nt(soft[0], back_stack[...])
    att_ref[...] = jnp.transpose(att_t[...]).astype(BF16)
    dq_ref[...] = jnp.transpose(dq_t[...]).astype(BF16)


def added(parts):
    total = parts[0][...].astype(F32)
    for part in parts[1:]:
        total = total + part[...].astype(F32)
    return total


def weights_kernel(
    cuts, head_ref, frames_ref, grads_ref, att_ref, own_ref, far1, far2, far3, pair_ref, other_pair_ref,
    kv_grad_ref, terms_ref, keep_ref, send_ref, held,
):
    outer, inner, tail = cuts
    rounded = added((own_ref, far1, far2, far3)).astype(BF16)
    kv_grad_ref[...] = rounded
    span = rounded.shape[1] // 2
    value_term = dot_tn(frames_ref[...], rounded[:, span:]).reshape(outer, inner, tail, span)
    out_term = dot_tn(grads_ref[...], att_ref[...]).reshape(outer, inner, tail, span)
    for i in range(inner):
        piece = jnp.stack([value_term[:, i], out_term[:, i]], axis=1)
        terms_ref[i] = piece.reshape(2 * outer * tail, span).astype(BF16)
    held[...] = added((pair_ref, other_pair_ref))
    chip = lax.shift_right_logical(head_ref[0], 1)
    half = keep_ref.shape[0]
    keep_ref[...] = held[pl.ds(pl.multiple_of(chip * half, half), half), :]
    send_ref[...] = held[pl.ds(pl.multiple_of((1 - chip) * half, half), half), :].astype(BF16)


def shares(head_ref, term, outs):
    half = outs[0].shape[0]
    for other, out in enumerate(outs):
        start = pl.multiple_of(jnp.bitwise_xor(head_ref[0], other) * half, half)
        out[...] = term[pl.ds(start, half), :].astype(BF16)


def mix_kernel(head_ref, att_ref, out_weight_ref, after_ref, keep_ref, send_ref, held):
    held[...] = dot_nn(att_ref[...], out_weight_ref[...])
    half = keep_ref.shape[0] // 2
    core = jnp.bitwise_and(head_ref[0], 1)
    for chip in range(2):
        rows = pl.ds(chip * half, half)
        start = pl.multiple_of((2 * chip + core) * half, half)
        keep_ref[rows, :] = held[pl.ds(start, half), :].astype(BF16)
        start = pl.multiple_of((2 * chip + 1 - core) * half, half)
        send_ref[rows, :] = held[pl.ds(start, half), :].astype(BF16)


def input_kernel(
    head_ref, dq_ref, kv_grad_ref, query_weight_ref, key_weight_ref, value_weight_ref,
    own_ref, send1, send2, send3, held,
):
    span = dq_ref.shape[1]
    term = dot_nt(dq_ref[...], query_weight_ref[...])
    term = term + dot_nt(kv_grad_ref[:, :span], key_weight_ref[...])
    held[...] = term + dot_nt(kv_grad_ref[:, span:], value_weight_ref[...])
    shares(head_ref, held, (own_ref, send1, send2, send3))


def near_kernel(pieces_ref, part0, part1, after_ref, terms_ref, mixed_ref):
    terms_ref[...] = added([pieces_ref.at[i] for i in range(pieces_ref.shape[0])]).astype(BF16)
    mixed_ref[...] = added((part0, part1)).astype(BF16)


def far_kernel(pieces_ref, value_ref, out_ref):
    total = added([pieces_ref.at[i] for i in range(pieces_ref.shape[0])])
    rows = value_ref.shape[0]
    value_ref[...] = total[:rows]
    out_ref[...] = total[rows:]


def head_sum_kernel(part0, part1, part2, part3, sum_ref):
    sum_ref[...] = added((part0, part1, part2, part3)).astype(BF16)


def passed_along(value, steps):
    count = lax.axis_size("seq")
    first, last = max(0, -steps), min(count, count - steps)
    return lax.ppermute(value, "seq", [(i, i + steps) for i in range(first, last)])


def with_head(value, other):
    return lax.ppermute(value, "head", [(i, i ^ other) for i in range(lax.axis_size("head"))])


def exchanged(sends):
    count = lax.axis_size("head")
    received = {}
    for other in range(count - 1, 0, -1):
        pairs = [(i, i ^ other) for i in range(count)]
        received[other] = lax.ppermute(sends[other - 1], "head", pairs)
    return [received[other] for other in range(1, count)]


def per_device(inner, frames_in, query_weight, key_weight, value_weight, out_weight, read_mask, out_grad):
    seq = lax.axis_size("seq")
    groups = lax.axis_size("head")
    outer = seq // inner
    width, span = query_weight.shape
    tail = width // seq
    near = [[o * inner + i for i in range(inner)] for o in range(outer)]
    across = [[o * inner + i for o in range(outer)] for i in range(inner)]
    mask = lax.dynamic_slice_in_dim(read_mask, lax.axis_index("seq"), 1, 0)
    group = jnp.full((1,), lax.axis_index("head"), jnp.int32)

    share = frames_in.shape[0]
    count = groups * share
    square = 2 * count * span
    heads = span // HEAD_DIM
    pairs = heads * WINDOW * count * count
    side = shape_of((span, count), BF16)
    kv_shape = shape_of((count, 2 * span), BF16)
    held = pltpu.VMEM((count, width), F32)

    frames = lax.all_gather(frames_in, "head", axis=0, tiled=True)
    [kv] = call(kv_kernel, [kv_shape], [frames, key_weight, value_weight], flops=2 * square * width)
    kvs = [kv] + [passed_along(kv, steps) for steps in range(1, WINDOW)]
    grads = lax.all_gather(out_grad, "head", axis=0, tiled=True)
    qt, bt = call(
        query_kernel,
        [side, side],
        [frames, grads, query_weight, out_weight],
        flops=2 * square * width,
    )
    attended, dq, own, *fars = call(
        attention_kernel,
        [shape_of((count, span), BF16)] * 2
        + [shape_of((count, 2 * span), F32)]
        + [kv_shape] * (WINDOW - 1),
        [mask, qt, bt, *kvs],
        [pltpu.VMEM((WINDOW, count, heads * count), BF16)] * 2
        + [pltpu.VMEM((span, heads * count), BF16)] * 2
        + [pltpu.VMEM((span, count), F32)] * 2,
        smem=1,
        flops=12 * pairs * span,
        transcendentals=pairs,
    )
    fars = [passed_along(fars[k - 1], -k) for k in range(1, WINDOW)]
    shared = shape_of((share, width), BF16)
    pair = shape_of((2 * share, width), BF16)
    pair_kept, pair_sent = call(
        mix_kernel,
        [pair, pair],
        [group, attended, out_weight, fars[0]],
        [held],
        smem=1,
        flops=square * width,
    )
    kv_grad, terms, mixed_kept, mixed_sent = call(
        functools.partial(weights_kernel, (outer, inner, tail)),
        [
            kv_shape,
            shape_of((inner, 2 * outer * tail, span), BF16),
            shape_of((share, width), F32),
            shared,
        ],
        [group, frames, grads, attended, own, *fars, pair_kept, with_head(pair_sent, 1)],
        [pltpu.VMEM((2 * share, width), F32)],
        smem=1,
        flops=2 * square * width,
    )
    mixed_received = with_head(mixed_sent, 2)
    terms = lax.all_to_all(terms, "seq", 0, 0, axis_index_groups=near, tiled=True)
    kept, *sends = call(
        input_kernel,
        [shared] * groups,
        [group, dq, kv_grad, query_weight, key_weight, value_weight],
        [held],
        smem=1,
        flops=3 * square * width,
    )
    terms, mixed = call(
        near_kernel,
        [shape_of((2 * outer * tail, span), BF16), shared],
        [terms, mixed_kept, mixed_received, kept],
    )
    terms = terms.reshape(outer, 2 * tail, span)
    terms = lax.all_to_all(terms, "seq", 0, 0, axis_index_groups=across, tiled=True)
    [frames_grad] = call(head_sum_kernel, [shared], [kept, *exchanged(sends)])
    value_sum, out_sum = call(far_kernel, [shape_of((tail, span), F32)] * 2, [terms])
    return mixed, frames_grad, value_sum, out_sum.T


def solution(mesh):
    in_specs = (
        P(("seq", "head"), None),
        P(None, "head"),
        P(None, "head"),
        P(None, "head"),
        P("head", None),
        P(),
        P(("seq", "head"), None),
    )
    out_specs = (
        P(("seq", "head"), None),
        P(("seq", "head"), None),
        P("seq", "head"),
        P("head", "seq"),
    )
    return jax.shard_map(
        functools.partial(per_device, min(8, mesh.shape["seq"])),
        mesh=mesh,
        in_specs=in_specs,
        out_specs=out_specs,
        check_vma=False,
    )
```

```python
import functools

import jax
import jax.numpy as jnp
from jax import lax
from jax.experimental import pallas as pl
from jax.experimental.pallas import tpu as pltpu
from jax.sharding import PartitionSpec as P

HEAD_DIM = 64
WINDOW = 4
FAR = 1e30
VMEM_LIMIT = 12 * 1024 * 1024

F32 = jnp.float32
BF16 = jnp.bfloat16


def dot_nn(left, right):
    return jnp.dot(left, right, preferred_element_type=F32)


def dot_nt(left, right):
    return lax.dot_general(left, right, (((1,), (1,)), ((), ())), preferred_element_type=F32)


def dot_tn(left, right):
    return lax.dot_general(left, right, (((0,), (0,)), ((), ())), preferred_element_type=F32)


def turned(array):
    return jnp.transpose(array.astype(F32)).astype(BF16)


def call(kernel, outs, operands, scratch=(), smem=0, flops=0, transcendentals=0):
    specs = [pl.BlockSpec(memory_space=pltpu.SMEM)] * smem
    specs += [pl.BlockSpec(memory_space=pltpu.VMEM)] * (len(operands) - smem)
    touched = sum(o.size * o.dtype.itemsize for o in (*operands, *outs))
    return pl.pallas_call(
        kernel,
        out_shape=outs,
        in_specs=specs,
        out_specs=[pl.BlockSpec(memory_space=pltpu.VMEM)] * len(outs),
        scratch_shapes=list(scratch),
        compiler_params=pltpu.CompilerParams(vmem_limit_bytes=VMEM_LIMIT),
        cost_estimate=pl.CostEstimate(
            flops=flops, bytes_accessed=touched, transcendentals=transcendentals
        ),
    )(*operands)


def shape_of(shape, dtype):
    return jax.ShapeDtypeStruct(shape, dtype)


def head_rows(array, head):
    rows = lax.broadcasted_iota(jnp.int32, array.shape, 0)
    inside = (rows >= head * HEAD_DIM) & (rows < (head + 1) * HEAD_DIM)
    return jnp.where(inside, array, jnp.zeros_like(array))


def kv_kernel(frames_ref, key_weight_ref, value_weight_ref, kv_ref):
    span = key_weight_ref.shape[1]
    kv_ref[:, :span] = dot_nn(frames_ref[...], key_weight_ref[...]).astype(BF16)
    kv_ref[:, span:] = dot_nn(frames_ref[...], value_weight_ref[...]).astype(BF16)


def query_kernel(frames_ref, grads_ref, query_weight_ref, out_weight_ref, qt_ref, back_ref):
    queries = dot_nn(frames_ref[...], query_weight_ref[...]).astype(BF16).astype(F32)
    qt_ref[...] = (jnp.transpose(queries) * (HEAD_DIM**-0.5)).astype(BF16)
    back_ref[...] = dot_nt(out_weight_ref[...], grads_ref[...]).astype(BF16)


def attention_kernel(
    mask_ref, qt_ref, bt_ref, kv0, kv1, kv2, kv3, att_ref, dq_ref, own_ref, far1, far2, far3,
    soft, grad, back_stack, query_stack, att_t, dq_t,
):
    kvs = (kv0, kv1, kv2, kv3)
    span, count = qt_ref.shape
    heads = span // HEAD_DIM
    keep = [None] + [mask_ref[0, k] > 0 for k in range(WINDOW - 1)]
    keys_t = [turned(kv[:, :span]) for kv in kvs]
    values_t = [turned(kv[:, span:]) for kv in kvs]
    for head in range(heads):
        mine = slice(head * HEAD_DIM, (head + 1) * HEAD_DIM)
        lanes = slice(head * count, (head + 1) * count)
        query = head_rows(qt_ref[...], head)
        back = head_rows(bt_ref[...], head)
        query_stack[:, lanes] = query
        back_stack[:, lanes] = back
        scores = [dot_nn(kv[:, :span], query) for kv in kvs]
        top = jnp.max(scores[0], axis=0, keepdims=True)
        for k in range(1, WINDOW):
            block_top = jnp.max(scores[k], axis=0, keepdims=True)
            top = jnp.maximum(top, jnp.where(keep[k], block_top, -FAR))
        raised = [jnp.exp(scores[0] - top)]
        for k in range(1, WINDOW):
            raised.append(jnp.exp(scores[k] - jnp.where(keep[k], top, FAR)))
        total = sum(jnp.sum(part, axis=0, keepdims=True) for part in raised)
        inverse = 1.0 / total
        weights = [part * inverse for part in raised]
        out = jnp.zeros((HEAD_DIM, count), F32)
        for k in range(WINDOW):
            rounded = weights[k].astype(BF16)
            soft[k, :, lanes] = rounded
            out = out + dot_nn(values_t[k][mine, :], rounded)
        out = out.astype(BF16).astype(F32)
        att_t[mine, :] = out
        back_dot = jnp.sum(out * bt_ref[mine, :].astype(F32), axis=0, keepdims=True)
        out = jnp.zeros((HEAD_DIM, count), F32)
        for k in range(WINDOW):
            back_scores = dot_nn(kvs[k][:, span:], back)
            score_grad = (weights[k] * (back_scores - back_dot)).astype(BF16)
            grad[k, :, lanes] = score_grad
            out = out + dot_nn(keys_t[k][mine, :], score_grad)
        dq_t[mine, :] = out * (HEAD_DIM**-0.5)
    for k, far in ((1, far1), (2, far2), (3, far3)):
        far[:, :span] = dot_nt(grad[k], query_stack[...]).astype(BF16)
        far[:, span:] = dot_nt(soft[k], back_stack[...]).astype(BF16)
    own_ref[:, :span] = dot_nt(grad[0], query_stack[...])
    own_ref[:, span:] = dot_nt(soft[0], back_stack[...])
    att_ref[...] = jnp.transpose(att_t[...]).astype(BF16)
    dq_ref[...] = jnp.transpose(dq_t[...]).astype(BF16)


def added(parts):
    total = parts[0][...].astype(F32)
    for part in parts[1:]:
        total = total + part[...].astype(F32)
    return total


def weights_kernel(
    cuts, head_ref, frames_ref, grads_ref, att_ref, own_ref, far1, far2, far3, pair_ref, other_pair_ref,
    kv_grad_ref, terms_ref, keep_ref, send_ref, held,
):
    outer, inner, tail = cuts
    rounded = added((own_ref, far1, far2, far3)).astype(BF16)
    kv_grad_ref[...] = rounded
    span = rounded.shape[1] // 2
    value_term = dot_tn(frames_ref[...], rounded[:, span:]).reshape(outer, inner, tail, span)
    out_term = dot_tn(grads_ref[...], att_ref[...]).reshape(outer, inner, tail, span)
    for i in range(inner):
        piece = jnp.stack([value_term[:, i], out_term[:, i]], axis=1)
        terms_ref[i] = piece.reshape(2 * outer * tail, span).astype(BF16)
    held[...] = added((pair_ref, other_pair_ref))
    chip = lax.shift_right_logical(head_ref[0], 1)
    half = keep_ref.shape[0]
    keep_ref[...] = held[pl.ds(pl.multiple_of(chip * half, half), half), :]
    send_ref[...] = held[pl.ds(pl.multiple_of((1 - chip) * half, half), half), :].astype(BF16)


def shares(head_ref, term, outs):
    half = outs[0].shape[0]
    for other, out in enumerate(outs):
        start = pl.multiple_of(jnp.bitwise_xor(head_ref[0], other) * half, half)
        out[...] = term[pl.ds(start, half), :].astype(BF16)


def mix_kernel(head_ref, att_ref, out_weight_ref, after_ref, keep_ref, send_ref, held):
    held[...] = dot_nn(att_ref[...], out_weight_ref[...])
    half = keep_ref.shape[0] // 2
    core = jnp.bitwise_and(head_ref[0], 1)
    for chip in range(2):
        rows = pl.ds(chip * half, half)
        start = pl.multiple_of((2 * chip + core) * half, half)
        keep_ref[rows, :] = held[pl.ds(start, half), :].astype(BF16)
        start = pl.multiple_of((2 * chip + 1 - core) * half, half)
        send_ref[rows, :] = held[pl.ds(start, half), :].astype(BF16)


def input_kernel(
    head_ref, dq_ref, kv_grad_ref, query_weight_ref, key_weight_ref, value_weight_ref,
    own_ref, send1, send2, send3, held,
):
    span = dq_ref.shape[1]
    term = dot_nt(dq_ref[...], query_weight_ref[...])
    term = term + dot_nt(kv_grad_ref[:, :span], key_weight_ref[...])
    held[...] = term + dot_nt(kv_grad_ref[:, span:], value_weight_ref[...])
    shares(head_ref, held, (own_ref, send1, send2, send3))


def near_kernel(pieces_ref, part0, part1, after_ref, terms_ref, mixed_ref):
    terms_ref[...] = added([pieces_ref.at[i] for i in range(pieces_ref.shape[0])]).astype(BF16)
    mixed_ref[...] = added((part0, part1)).astype(BF16)


def far_kernel(pieces_ref, value_ref, out_ref):
    total = added([pieces_ref.at[i] for i in range(pieces_ref.shape[0])])
    rows = value_ref.shape[0]
    value_ref[...] = total[:rows]
    out_ref[...] = total[rows:]


def head_sum_kernel(part0, part1, part2, part3, sum_ref):
    sum_ref[...] = added((part0, part1, part2, part3)).astype(BF16)


def passed_along(value, steps):
    count = lax.axis_size("seq")
    first, last = max(0, -steps), min(count, count - steps)
    return lax.ppermute(value, "seq", [(i, i + steps) for i in range(first, last)])


def with_head(value, other):
    return lax.ppermute(value, "head", [(i, i ^ other) for i in range(lax.axis_size("head"))])


def per_device(inner, frames_in, query_weight, key_weight, value_weight, out_weight, read_mask, out_grad):
    seq = lax.axis_size("seq")
    groups = lax.axis_size("head")
    outer = seq // inner
    width, span = query_weight.shape
    tail = width // seq
    near = [[o * inner + i for i in range(inner)] for o in range(outer)]
    across = [[o * inner + i for o in range(outer)] for i in range(inner)]
    mask = lax.dynamic_slice_in_dim(read_mask, lax.axis_index("seq"), 1, 0)
    group = jnp.full((1,), lax.axis_index("head"), jnp.int32)

    share = frames_in.shape[0]
    count = groups * share
    square = 2 * count * span
    heads = span // HEAD_DIM
    pairs = heads * WINDOW * count * count
    side = shape_of((span, count), BF16)
    kv_shape = shape_of((count, 2 * span), BF16)
    held = pltpu.VMEM((count, width), F32)

    frames = lax.all_gather(frames_in, "head", axis=0, tiled=True)
    [kv] = call(kv_kernel, [kv_shape], [frames, key_weight, value_weight], flops=2 * square * width)
    kvs = [kv] + [passed_along(kv, steps) for steps in range(1, WINDOW)]
    grads = lax.all_gather(out_grad, "head", axis=0, tiled=True)
    qt, bt = call(
        query_kernel,
        [side, side],
        [frames, grads, query_weight, out_weight],
        flops=2 * square * width,
    )
    attended, dq, own, *fars = call(
        attention_kernel,
        [shape_of((count, span), BF16)] * 2
        + [shape_of((count, 2 * span), F32)]
        + [kv_shape] * (WINDOW - 1),
        [mask, qt, bt, *kvs],
        [pltpu.VMEM((WINDOW, count, heads * count), BF16)] * 2
        + [pltpu.VMEM((span, heads * count), BF16)] * 2
        + [pltpu.VMEM((span, count), F32)] * 2,
        smem=1,
        flops=12 * pairs * span,
        transcendentals=pairs,
    )
    fars = [passed_along(fars[k - 1], -k) for k in range(1, WINDOW)]
    shared = shape_of((share, width), BF16)
    pair = shape_of((2 * share, width), BF16)
    pair_kept, pair_sent = call(
        mix_kernel,
        [pair, pair],
        [group, attended, out_weight, fars[0]],
        [held],
        smem=1,
        flops=square * width,
    )
    kv_grad, terms, mixed_kept, mixed_sent = call(
        functools.partial(weights_kernel, (outer, inner, tail)),
        [
            kv_shape,
            shape_of((inner, 2 * outer * tail, span), BF16),
            shape_of((share, width), F32),
            shared,
        ],
        [group, frames, grads, attended, own, *fars, pair_kept, with_head(pair_sent, 1)],
        [pltpu.VMEM((2 * share, width), F32)],
        smem=1,
        flops=2 * square * width,
    )
    mixed_received = with_head(mixed_sent, 2)
    terms = lax.all_to_all(terms, "seq", 0, 0, axis_index_groups=near, tiled=True)
    kept, *sends = call(
        input_kernel,
        [shared] * groups,
        [group, dq, kv_grad, query_weight, key_weight, value_weight],
        [held],
        smem=1,
        flops=3 * square * width,
    )
    received = [with_head(sends[0], 1)]
    terms, mixed = call(
        near_kernel,
        [shape_of((2 * outer * tail, span), BF16), shared],
        [terms, mixed_kept, mixed_received, received[0]],
    )
    terms = terms.reshape(outer, 2 * tail, span)
    terms = lax.all_to_all(terms, "seq", 0, 0, axis_index_groups=across, tiled=True)
    received += [with_head(sends[other - 1], other) for other in range(2, groups)]
    [frames_grad] = call(head_sum_kernel, [shared], [kept, *received])
    value_sum, out_sum = call(far_kernel, [shape_of((tail, span), F32)] * 2, [terms])
    return mixed, frames_grad, value_sum, out_sum.T


def solution(mesh):
    in_specs = (
        P(("seq", "head"), None),
        P(None, "head"),
        P(None, "head"),
        P(None, "head"),
        P("head", None),
        P(),
        P(("seq", "head"), None),
    )
    out_specs = (
        P(("seq", "head"), None),
        P(("seq", "head"), None),
        P("seq", "head"),
        P("head", "seq"),
    )
    return jax.shard_map(
        functools.partial(per_device, min(8, mesh.shape["seq"])),
        mesh=mesh,
        in_specs=in_specs,
        out_specs=out_specs,
        check_vma=False,
    )
```

```python
import functools

import jax
import jax.numpy as jnp
from jax import lax
from jax.experimental import pallas as pl
from jax.experimental.pallas import tpu as pltpu
from jax.sharding import PartitionSpec as P

HEAD_DIM = 64
WINDOW = 4
FAR = 1e30
VMEM_LIMIT = 12 * 1024 * 1024

F32 = jnp.float32
BF16 = jnp.bfloat16


def dot_nn(left, right):
    return jnp.dot(left, right, preferred_element_type=F32)


def dot_nt(left, right):
    return lax.dot_general(left, right, (((1,), (1,)), ((), ())), preferred_element_type=F32)


def dot_tn(left, right):
    return lax.dot_general(left, right, (((0,), (0,)), ((), ())), preferred_element_type=F32)


def turned(array):
    return jnp.transpose(array.astype(F32)).astype(BF16)


def call(kernel, outs, operands, scratch=(), smem=0, flops=0, transcendentals=0):
    specs = [pl.BlockSpec(memory_space=pltpu.SMEM)] * smem
    specs += [pl.BlockSpec(memory_space=pltpu.VMEM)] * (len(operands) - smem)
    touched = sum(o.size * o.dtype.itemsize for o in (*operands, *outs))
    return pl.pallas_call(
        kernel,
        out_shape=outs,
        in_specs=specs,
        out_specs=[pl.BlockSpec(memory_space=pltpu.VMEM)] * len(outs),
        scratch_shapes=list(scratch),
        compiler_params=pltpu.CompilerParams(vmem_limit_bytes=VMEM_LIMIT),
        cost_estimate=pl.CostEstimate(
            flops=flops, bytes_accessed=touched, transcendentals=transcendentals
        ),
    )(*operands)


def shape_of(shape, dtype):
    return jax.ShapeDtypeStruct(shape, dtype)


def head_rows(array, head):
    rows = lax.broadcasted_iota(jnp.int32, array.shape, 0)
    inside = (rows >= head * HEAD_DIM) & (rows < (head + 1) * HEAD_DIM)
    return jnp.where(inside, array, jnp.zeros_like(array))


def kv_kernel(frames_ref, key_weight_ref, value_weight_ref, kv_ref):
    span = key_weight_ref.shape[1]
    kv_ref[:, :span] = dot_nn(frames_ref[...], key_weight_ref[...]).astype(BF16)
    kv_ref[:, span:] = dot_nn(frames_ref[...], value_weight_ref[...]).astype(BF16)


def query_kernel(frames_ref, grads_ref, query_weight_ref, out_weight_ref, qt_ref, back_ref):
    queries = dot_nn(frames_ref[...], query_weight_ref[...]).astype(BF16).astype(F32)
    qt_ref[...] = (jnp.transpose(queries) * (HEAD_DIM**-0.5)).astype(BF16)
    back_ref[...] = dot_nt(out_weight_ref[...], grads_ref[...]).astype(BF16)


def attention_kernel(
    mask_ref, qt_ref, bt_ref, kv0, kv1, kv2, kv3, att_ref, dq_ref, own_ref, far1, far2, far3,
    soft, grad, back_stack, query_stack, att_t, dq_t,
):
    kvs = (kv0, kv1, kv2, kv3)
    span, count = qt_ref.shape
    heads = span // HEAD_DIM
    keep = [None] + [mask_ref[0, k] > 0 for k in range(WINDOW - 1)]
    keys_t = [turned(kv[:, :span]) for kv in kvs]
    values_t = [turned(kv[:, span:]) for kv in kvs]
    for head in range(heads):
        mine = slice(head * HEAD_DIM, (head + 1) * HEAD_DIM)
        lanes = slice(head * count, (head + 1) * count)
        query = head_rows(qt_ref[...], head)
        back = head_rows(bt_ref[...], head)
        query_stack[:, lanes] = query
        back_stack[:, lanes] = back
        scores = [dot_nn(kv[:, :span], query) for kv in kvs]
        top = jnp.max(scores[0], axis=0, keepdims=True)
        for k in range(1, WINDOW):
            block_top = jnp.max(scores[k], axis=0, keepdims=True)
            top = jnp.maximum(top, jnp.where(keep[k], block_top, -FAR))
        raised = [jnp.exp(scores[0] - top)]
        for k in range(1, WINDOW):
            raised.append(jnp.exp(scores[k] - jnp.where(keep[k], top, FAR)))
        total = sum(jnp.sum(part, axis=0, keepdims=True) for part in raised)
        inverse = 1.0 / total
        weights = [part * inverse for part in raised]
        out = jnp.zeros((HEAD_DIM, count), F32)
        for k in range(WINDOW):
            rounded = weights[k].astype(BF16)
            soft[k, :, lanes] = rounded
            out = out + dot_nn(values_t[k][mine, :], rounded)
        out = out.astype(BF16).astype(F32)
        att_t[mine, :] = out
        back_dot = jnp.sum(out * bt_ref[mine, :].astype(F32), axis=0, keepdims=True)
        out = jnp.zeros((HEAD_DIM, count), F32)
        for k in range(WINDOW):
            back_scores = dot_nn(kvs[k][:, span:], back)
            score_grad = (weights[k] * (back_scores - back_dot)).astype(BF16)
            grad[k, :, lanes] = score_grad
            out = out + dot_nn(keys_t[k][mine, :], score_grad)
        dq_t[mine, :] = out * (HEAD_DIM**-0.5)
    for k, far in ((1, far1), (2, far2), (3, far3)):
        far[:, :span] = dot_nt(grad[k], query_stack[...]).astype(BF16)
        far[:, span:] = dot_nt(soft[k], back_stack[...]).astype(BF16)
    own_ref[:, :span] = dot_nt(grad[0], query_stack[...])
    own_ref[:, span:] = dot_nt(soft[0], back_stack[...])
    att_ref[...] = jnp.transpose(att_t[...]).astype(BF16)
    dq_ref[...] = jnp.transpose(dq_t[...]).astype(BF16)


def added(parts):
    total = parts[0][...].astype(F32)
    for part in parts[1:]:
        total = total + part[...].astype(F32)
    return total


def weights_kernel(cuts, frames_ref, grads_ref, att_ref, own_ref, far1, far2, far3, kv_grad_ref, terms_ref):
    outer, inner, tail = cuts
    rounded = added((own_ref, far1, far2, far3)).astype(BF16)
    kv_grad_ref[...] = rounded
    span = rounded.shape[1] // 2
    value_term = dot_tn(frames_ref[...], rounded[:, span:]).reshape(outer, inner, tail, span)
    out_term = dot_tn(grads_ref[...], att_ref[...]).reshape(outer, inner, tail, span)
    for i in range(inner):
        piece = jnp.stack([value_term[:, i], out_term[:, i]], axis=1)
        terms_ref[i] = piece.reshape(2 * outer * tail, span).astype(BF16)


def shares(head_ref, term, outs):
    half = outs[0].shape[0]
    for other, out in enumerate(outs):
        start = pl.multiple_of(jnp.bitwise_xor(head_ref[0], other) * half, half)
        out[...] = term[pl.ds(start, half), :].astype(BF16)


def input_kernel(
    head_ref, dq_ref, kv_grad_ref, query_weight_ref, key_weight_ref, value_weight_ref, att_ref, out_weight_ref,
    own_ref, send1, send2, send3, pair_ref, held_mixed, held,
):
    span = dq_ref.shape[1]
    held_mixed[...] = dot_nn(att_ref[...], out_weight_ref[...])
    term = dot_nt(dq_ref[...], query_weight_ref[...])
    term = term + dot_nt(kv_grad_ref[:, :span], key_weight_ref[...])
    held[...] = term + dot_nt(kv_grad_ref[:, span:], value_weight_ref[...])
    half = own_ref.shape[0]
    shares(head_ref, held, (own_ref, send1.at[pl.ds(0, half), :], send2, send3))
    core = jnp.bitwise_and(head_ref[0], 1)
    for chip in range(2):
        start = pl.multiple_of((2 * chip + core) * half, half)
        pair_ref[pl.ds(chip * half, half), :] = held_mixed[pl.ds(start, half), :].astype(BF16)
        start = pl.multiple_of((2 * chip + 1 - core) * half, half)
        send1[pl.ds((1 + chip) * half, half), :] = held_mixed[pl.ds(start, half), :].astype(BF16)


def near_kernel(
    head_ref, pieces_ref, own_ref, pair_ref, from1, from3, frames_send_ref, terms_ref, part_ref, send2, held
):
    terms_ref[...] = added([pieces_ref.at[i] for i in range(pieces_ref.shape[0])]).astype(BF16)
    half = own_ref.shape[0]
    held[...] = added((pair_ref, from1.at[pl.ds(half, 2 * half), :]))
    chip = lax.shift_right_logical(head_ref[0], 1)
    part_ref[pl.ds(0, half), :] = added((own_ref, from1.at[pl.ds(0, half), :], from3))
    part_ref[pl.ds(half, half), :] = held[pl.ds(pl.multiple_of(chip * half, half), half), :]
    send2[pl.ds(0, half), :] = frames_send_ref[...]
    mixed_send = held[pl.ds(pl.multiple_of((1 - chip) * half, half), half), :]
    send2[pl.ds(half, half), :] = mixed_send.astype(BF16)


def far_kernel(pieces_ref, value_ref, out_ref):
    total = added([pieces_ref.at[i] for i in range(pieces_ref.shape[0])])
    rows = value_ref.shape[0]
    value_ref[...] = total[:rows]
    out_ref[...] = total[rows:]


def head_sum_kernel(part_ref, from2, frames_grad_ref, mixed_ref):
    total = added((part_ref, from2))
    half = mixed_ref.shape[0]
    frames_grad_ref[...] = total[:half].astype(BF16)
    mixed_ref[...] = total[half:].astype(BF16)


def passed_along(value, steps):
    count = lax.axis_size("seq")
    first, last = max(0, -steps), min(count, count - steps)
    return lax.ppermute(value, "seq", [(i, i + steps) for i in range(first, last)])


def with_head(value, other):
    return lax.ppermute(value, "head", [(i, i ^ other) for i in range(lax.axis_size("head"))])


def per_device(inner, frames_in, query_weight, key_weight, value_weight, out_weight, read_mask, out_grad):
    seq = lax.axis_size("seq")
    groups = lax.axis_size("head")
    outer = seq // inner
    width, span = query_weight.shape
    tail = width // seq
    near = [[o * inner + i for i in range(inner)] for o in range(outer)]
    across = [[o * inner + i for o in range(outer)] for i in range(inner)]
    mask = lax.dynamic_slice_in_dim(read_mask, lax.axis_index("seq"), 1, 0)
    group = jnp.full((1,), lax.axis_index("head"), jnp.int32)

    share = frames_in.shape[0]
    count = groups * share
    square = 2 * count * span
    heads = span // HEAD_DIM
    pairs = heads * WINDOW * count * count
    side = shape_of((span, count), BF16)
    kv_shape = shape_of((count, 2 * span), BF16)
    held = pltpu.VMEM((count, width), F32)

    frames = lax.all_gather(frames_in, "head", axis=0, tiled=True)
    [kv] = call(kv_kernel, [kv_shape], [frames, key_weight, value_weight], flops=2 * square * width)
    kvs = [kv] + [passed_along(kv, steps) for steps in range(1, WINDOW)]
    grads = lax.all_gather(out_grad, "head", axis=0, tiled=True)
    qt, bt = call(
        query_kernel,
        [side, side],
        [frames, grads, query_weight, out_weight],
        flops=2 * square * width,
    )
    attended, dq, own, *fars = call(
        attention_kernel,
        [shape_of((count, span), BF16)] * 2
        + [shape_of((count, 2 * span), F32)]
        + [kv_shape] * (WINDOW - 1),
        [mask, qt, bt, *kvs],
        [pltpu.VMEM((WINDOW, count, heads * count), BF16)] * 2
        + [pltpu.VMEM((span, heads * count), BF16)] * 2
        + [pltpu.VMEM((span, count), F32)] * 2,
        smem=1,
        flops=12 * pairs * span,
        transcendentals=pairs,
    )
    fars = [passed_along(fars[k - 1], -k) for k in range(1, WINDOW)]
    kv_grad, terms = call(
        functools.partial(weights_kernel, (outer, inner, tail)),
        [kv_shape, shape_of((inner, 2 * outer * tail, span), BF16)],
        [frames, grads, attended, own, *fars],
        flops=2 * square * width,
    )
    terms = lax.all_to_all(terms, "seq", 0, 0, axis_index_groups=near, tiled=True)
    shared = shape_of((share, width), BF16)
    own, send1, send2, send3, pair = call(
        input_kernel,
        [
            shared,
            shape_of((3 * share, width), BF16),
            shared,
            shared,
            shape_of((2 * share, width), BF16),
        ],
        [group, dq, kv_grad, query_weight, key_weight, value_weight, attended, out_weight],
        [held, held],
        smem=1,
        flops=4 * square * width,
    )
    terms, part, send2 = call(
        near_kernel,
        [
            shape_of((2 * outer * tail, span), BF16),
            shape_of((2 * share, width), F32),
            shape_of((2 * share, width), BF16),
        ],
        [group, terms, own, pair, with_head(send1, 1), with_head(send3, 3), send2],
        [pltpu.VMEM((2 * share, width), F32)],
        smem=1,
    )
    terms = terms.reshape(outer, 2 * tail, span)
    terms = lax.all_to_all(terms, "seq", 0, 0, axis_index_groups=across, tiled=True)
    frames_grad, mixed = call(head_sum_kernel, [shared, shared], [part, with_head(send2, 2)])
    value_sum, out_sum = call(far_kernel, [shape_of((tail, span), F32)] * 2, [terms])
    return mixed, frames_grad, value_sum, out_sum.T


def solution(mesh):
    in_specs = (
        P(("seq", "head"), None),
        P(None, "head"),
        P(None, "head"),
        P(None, "head"),
        P("head", None),
        P(),
        P(("seq", "head"), None),
    )
    out_specs = (
        P(("seq", "head"), None),
        P(("seq", "head"), None),
        P("seq", "head"),
        P("head", "seq"),
    )
    return jax.shard_map(
        functools.partial(per_device, min(8, mesh.shape["seq"])),
        mesh=mesh,
        in_specs=in_specs,
        out_specs=out_specs,
        check_vma=False,
    )
```

```python
import functools

import jax
import jax.numpy as jnp
from jax import lax
from jax.experimental import pallas as pl
from jax.experimental.pallas import tpu as pltpu
from jax.sharding import PartitionSpec as P

HEAD_DIM = 64
WINDOW = 4
FAR = 1e30
VMEM_LIMIT = 12 * 1024 * 1024

F32 = jnp.float32
BF16 = jnp.bfloat16


def dot_nn(left, right):
    return jnp.dot(left, right, preferred_element_type=F32)


def dot_nt(left, right):
    return lax.dot_general(left, right, (((1,), (1,)), ((), ())), preferred_element_type=F32)


def dot_tn(left, right):
    return lax.dot_general(left, right, (((0,), (0,)), ((), ())), preferred_element_type=F32)


def turned(array):
    return jnp.transpose(array.astype(F32)).astype(BF16)


def call(kernel, outs, operands, scratch=(), smem=0, flops=0, transcendentals=0):
    specs = [pl.BlockSpec(memory_space=pltpu.SMEM)] * smem
    specs += [pl.BlockSpec(memory_space=pltpu.VMEM)] * (len(operands) - smem)
    touched = sum(o.size * o.dtype.itemsize for o in (*operands, *outs))
    return pl.pallas_call(
        kernel,
        out_shape=outs,
        in_specs=specs,
        out_specs=[pl.BlockSpec(memory_space=pltpu.VMEM)] * len(outs),
        scratch_shapes=list(scratch),
        compiler_params=pltpu.CompilerParams(vmem_limit_bytes=VMEM_LIMIT),
        cost_estimate=pl.CostEstimate(
            flops=flops, bytes_accessed=touched, transcendentals=transcendentals
        ),
    )(*operands)


def shape_of(shape, dtype):
    return jax.ShapeDtypeStruct(shape, dtype)


def head_rows(array, head):
    rows = lax.broadcasted_iota(jnp.int32, array.shape, 0)
    inside = (rows >= head * HEAD_DIM) & (rows < (head + 1) * HEAD_DIM)
    return jnp.where(inside, array, jnp.zeros_like(array))


def kv_kernel(frames_ref, key_weight_ref, value_weight_ref, kv_ref):
    span = key_weight_ref.shape[1]
    kv_ref[:, :span] = dot_nn(frames_ref[...], key_weight_ref[...]).astype(BF16)
    kv_ref[:, span:] = dot_nn(frames_ref[...], value_weight_ref[...]).astype(BF16)


def query_kernel(frames_ref, grads_ref, query_weight_ref, out_weight_ref, qt_ref, back_ref):
    queries = dot_nn(frames_ref[...], query_weight_ref[...]).astype(BF16).astype(F32)
    qt_ref[...] = (jnp.transpose(queries) * (HEAD_DIM**-0.5)).astype(BF16)
    back_ref[...] = dot_nt(out_weight_ref[...], grads_ref[...]).astype(BF16)


def attention_kernel(
    mask_ref, qt_ref, bt_ref, kv0, kv1, kv2, kv3, att_ref, dq_ref, own_ref, far1, far2, far3,
    soft, grad, back_stack, query_stack, att_t, dq_t,
):
    kvs = (kv0, kv1, kv2, kv3)
    span, count = qt_ref.shape
    heads = span // HEAD_DIM
    keep = [None] + [mask_ref[0, k] > 0 for k in range(WINDOW - 1)]
    keys_t = [turned(kv[:, :span]) for kv in kvs]
    values_t = [turned(kv[:, span:]) for kv in kvs]
    for head in range(heads):
        mine = slice(head * HEAD_DIM, (head + 1) * HEAD_DIM)
        lanes = slice(head * count, (head + 1) * count)
        query = head_rows(qt_ref[...], head)
        back = head_rows(bt_ref[...], head)
        query_stack[:, lanes] = query
        back_stack[:, lanes] = back
        scores = [dot_nn(kv[:, :span], query) for kv in kvs]
        top = jnp.max(scores[0], axis=0, keepdims=True)
        for k in range(1, WINDOW):
            block_top = jnp.max(scores[k], axis=0, keepdims=True)
            top = jnp.maximum(top, jnp.where(keep[k], block_top, -FAR))
        raised = [jnp.exp(scores[0] - top)]
        for k in range(1, WINDOW):
            raised.append(jnp.exp(scores[k] - jnp.where(keep[k], top, FAR)))
        total = sum(jnp.sum(part, axis=0, keepdims=True) for part in raised)
        inverse = 1.0 / total
        weights = [part * inverse for part in raised]
        out = jnp.zeros((HEAD_DIM, count), F32)
        for k in range(WINDOW):
            rounded = weights[k].astype(BF16)
            soft[k, :, lanes] = rounded
            out = out + dot_nn(values_t[k][mine, :], rounded)
        out = out.astype(BF16).astype(F32)
        att_t[mine, :] = out
        back_dot = jnp.sum(out * bt_ref[mine, :].astype(F32), axis=0, keepdims=True)
        out = jnp.zeros((HEAD_DIM, count), F32)
        for k in range(WINDOW):
            back_scores = dot_nn(kvs[k][:, span:], back)
            score_grad = (weights[k] * (back_scores - back_dot)).astype(BF16)
            grad[k, :, lanes] = score_grad
            out = out + dot_nn(keys_t[k][mine, :], score_grad)
        dq_t[mine, :] = out * (HEAD_DIM**-0.5)
    for k, far in ((1, far1), (2, far2), (3, far3)):
        far[:, :span] = dot_nt(grad[k], query_stack[...]).astype(BF16)
        far[:, span:] = dot_nt(soft[k], back_stack[...]).astype(BF16)
    own_ref[:, :span] = dot_nt(grad[0], query_stack[...])
    own_ref[:, span:] = dot_nt(soft[0], back_stack[...])
    att_ref[...] = jnp.transpose(att_t[...]).astype(BF16)
    dq_ref[...] = jnp.transpose(dq_t[...]).astype(BF16)


def added(parts):
    total = parts[0][...].astype(F32)
    for part in parts[1:]:
        total = total + part[...].astype(F32)
    return total


def weights_kernel(
    cuts, frames_ref, grads_ref, att_ref, dq_ref, own_ref, far1, far2, far3, kv_grad_ref, terms_ref
):
    outer, inner, tail = cuts
    rounded = added((own_ref, far1, far2, far3)).astype(BF16)
    span = rounded.shape[1] // 2
    kv_grad_ref[:, : 2 * span] = rounded
    kv_grad_ref[:, 2 * span :] = dq_ref[...]
    value_term = dot_tn(frames_ref[...], rounded[:, span:]).reshape(outer, inner, tail, span)
    out_term = dot_tn(grads_ref[...], att_ref[...]).reshape(outer, inner, tail, span)
    for i in range(inner):
        piece = jnp.stack([value_term[:, i], out_term[:, i]], axis=1)
        terms_ref[i] = piece.reshape(2 * outer * tail, span).astype(BF16)


def shares(head_ref, term, outs):
    half = outs[0].shape[0]
    for other, out in enumerate(outs):
        start = pl.multiple_of(jnp.bitwise_xor(head_ref[0], other) * half, half)
        out[...] = term[pl.ds(start, half), :].astype(BF16)


def input_kernel(
    head_ref, kv_grad_ref, query_weight_ref, key_weight_ref, value_weight_ref, att_ref, out_weight_ref,
    own_ref, send1, send2, send3, pair_ref, held_mixed, held,
):
    span = query_weight_ref.shape[1]
    held_mixed[...] = dot_nn(att_ref[...], out_weight_ref[...])
    term = dot_nt(kv_grad_ref[:, 2 * span :], query_weight_ref[...])
    term = term + dot_nt(kv_grad_ref[:, :span], key_weight_ref[...])
    held[...] = term + dot_nt(kv_grad_ref[:, span : 2 * span], value_weight_ref[...])
    half = own_ref.shape[0]
    shares(head_ref, held, (own_ref, send1.at[pl.ds(0, half), :], send2, send3))
    core = jnp.bitwise_and(head_ref[0], 1)
    for chip in range(2):
        start = pl.multiple_of((2 * chip + core) * half, half)
        pair_ref[pl.ds(chip * half, half), :] = held_mixed[pl.ds(start, half), :].astype(BF16)
        start = pl.multiple_of((2 * chip + 1 - core) * half, half)
        send1[pl.ds((1 + chip) * half, half), :] = held_mixed[pl.ds(start, half), :].astype(BF16)


def near_kernel(
    head_ref, pieces_ref, own_ref, pair_ref, from1, from3, frames_send_ref, terms_ref, part_ref, send2, held
):
    terms_ref[...] = added([pieces_ref.at[i] for i in range(pieces_ref.shape[0])]).astype(BF16)
    half = own_ref.shape[0]
    held[...] = added((pair_ref, from1.at[pl.ds(half, 2 * half), :]))
    chip = lax.shift_right_logical(head_ref[0], 1)
    part_ref[pl.ds(0, half), :] = added((own_ref, from1.at[pl.ds(0, half), :], from3))
    part_ref[pl.ds(half, half), :] = held[pl.ds(pl.multiple_of(chip * half, half), half), :]
    send2[pl.ds(0, half), :] = frames_send_ref[...]
    mixed_send = held[pl.ds(pl.multiple_of((1 - chip) * half, half), half), :]
    send2[pl.ds(half, half), :] = mixed_send.astype(BF16)


def far_kernel(pieces_ref, value_ref, out_ref):
    total = added([pieces_ref.at[i] for i in range(pieces_ref.shape[0])])
    rows = value_ref.shape[0]
    value_ref[...] = total[:rows]
    out_ref[...] = total[rows:]


def head_sum_kernel(part_ref, from2, frames_grad_ref, mixed_ref):
    total = added((part_ref, from2))
    half = mixed_ref.shape[0]
    frames_grad_ref[...] = total[:half].astype(BF16)
    mixed_ref[...] = total[half:].astype(BF16)


def passed_along(value, steps):
    count = lax.axis_size("seq")
    first, last = max(0, -steps), min(count, count - steps)
    return lax.ppermute(value, "seq", [(i, i + steps) for i in range(first, last)])


def with_head(value, other):
    return lax.ppermute(value, "head", [(i, i ^ other) for i in range(lax.axis_size("head"))])


def per_device(inner, frames_in, query_weight, key_weight, value_weight, out_weight, read_mask, out_grad):
    seq = lax.axis_size("seq")
    groups = lax.axis_size("head")
    outer = seq // inner
    width, span = query_weight.shape
    tail = width // seq
    near = [[o * inner + i for i in range(inner)] for o in range(outer)]
    across = [[o * inner + i for o in range(outer)] for i in range(inner)]
    mask = lax.dynamic_slice_in_dim(read_mask, lax.axis_index("seq"), 1, 0)
    group = jnp.full((1,), lax.axis_index("head"), jnp.int32)

    share = frames_in.shape[0]
    count = groups * share
    square = 2 * count * span
    heads = span // HEAD_DIM
    pairs = heads * WINDOW * count * count
    side = shape_of((span, count), BF16)
    kv_shape = shape_of((count, 2 * span), BF16)
    held = pltpu.VMEM((count, width), F32)

    frames = lax.all_gather(frames_in, "head", axis=0, tiled=True)
    [kv] = call(kv_kernel, [kv_shape], [frames, key_weight, value_weight], flops=2 * square * width)
    kvs = [kv] + [passed_along(kv, steps) for steps in range(1, WINDOW)]
    grads = lax.all_gather(out_grad, "head", axis=0, tiled=True)
    qt, bt = call(
        query_kernel,
        [side, side],
        [frames, grads, query_weight, out_weight],
        flops=2 * square * width,
    )
    attended, dq, own, *fars = call(
        attention_kernel,
        [shape_of((count, span), BF16)] * 2
        + [shape_of((count, 2 * span), F32)]
        + [kv_shape] * (WINDOW - 1),
        [mask, qt, bt, *kvs],
        [pltpu.VMEM((WINDOW, count, heads * count), BF16)] * 2
        + [pltpu.VMEM((span, heads * count), BF16)] * 2
        + [pltpu.VMEM((span, count), F32)] * 2,
        smem=1,
        flops=12 * pairs * span,
        transcendentals=pairs,
    )
    fars = [passed_along(fars[k - 1], -k) for k in range(1, WINDOW)]
    kv_grad, terms = call(
        functools.partial(weights_kernel, (outer, inner, tail)),
        [shape_of((count, 3 * span), BF16), shape_of((inner, 2 * outer * tail, span), BF16)],
        [frames, grads, attended, dq, own, *fars],
        flops=2 * square * width,
    )
    terms = lax.all_to_all(terms, "seq", 0, 0, axis_index_groups=near, tiled=True)
    shared = shape_of((share, width), BF16)
    own, send1, send2, send3, pair = call(
        input_kernel,
        [
            shared,
            shape_of((3 * share, width), BF16),
            shared,
            shared,
            shape_of((2 * share, width), BF16),
        ],
        [group, kv_grad, query_weight, key_weight, value_weight, attended, out_weight],
        [held, held],
        smem=1,
        flops=4 * square * width,
    )
    terms, part, send2 = call(
        near_kernel,
        [
            shape_of((2 * outer * tail, span), BF16),
            shape_of((2 * share, width), F32),
            shape_of((2 * share, width), BF16),
        ],
        [group, terms, own, pair, with_head(send1, 1), with_head(send3, 3), send2],
        [pltpu.VMEM((2 * share, width), F32)],
        smem=1,
    )
    terms = terms.reshape(outer, 2 * tail, span)
    terms = lax.all_to_all(terms, "seq", 0, 0, axis_index_groups=across, tiled=True)
    frames_grad, mixed = call(head_sum_kernel, [shared, shared], [part, with_head(send2, 2)])
    value_sum, out_sum = call(far_kernel, [shape_of((tail, span), F32)] * 2, [terms])
    return mixed, frames_grad, value_sum, out_sum.T


def solution(mesh):
    in_specs = (
        P(("seq", "head"), None),
        P(None, "head"),
        P(None, "head"),
        P(None, "head"),
        P("head", None),
        P(),
        P(("seq", "head"), None),
    )
    out_specs = (
        P(("seq", "head"), None),
        P(("seq", "head"), None),
        P("seq", "head"),
        P("head", "seq"),
    )
    return jax.shard_map(
        functools.partial(per_device, min(8, mesh.shape["seq"])),
        mesh=mesh,
        in_specs=in_specs,
        out_specs=out_specs,
        check_vma=False,
    )
```
